512 devices in a mesh: row: 8 (over x_lo, y), col: 64 (over x_hi, z, core).
Axes of the slice: x: 4 (x_hi: 2, x_lo: 2; x = x_hi * 2 + x_lo), y: 4, z: 16, core: 2. Of those that a mesh axis runs over, the one named last changes fastest.
Arguments:
- right_side: float32 [8192, 16384], P('row', 'col'), may hold values from -8 to 8
- factor_panels: float32 [4, 256, 8192], P(None, 'col', 'row'), may hold values from -0.1875 to 0.1875
- inverses: float32 [4, 256, 256], P(None, 'col'), may hold values from -0.5 to 1.6, as said below
Outputs:
- solved: float32 [8192, 16384], P('row', 'col')
The draws below stay inside these ranges and needn't reach their ends.
Inputs may be any that keep to these rules, and one draw needn't show every extreme that they name: inverses[k] is lower triangular with a diagonal between 0.6 and 1.6 and independent entries below it.
All inputs are finite; a program needn't handle non-finite values.
Results may differ from the reference program's by a relative error of at most 0.0001.
Values sent between devices are 32-bit elements; how exact they have to be, the bound alone decides.
A program may use at most 64 MiB of HBM per device.

```python
import jax
import jax.numpy as jnp
from jax import lax

NB = 256
PANELS = 4
ROW_DEV = 1024
RHS_DEV = 256
ROWS = 8192
RHS = 16384
N_ROW = 8


def draw_inverses(key, part):
    first, second = jax.random.split(jax.random.fold_in(key, 7))
    diagonal = jax.random.uniform(first, (PANELS, NB), jnp.float32, 0.6, 1.6)
    below = jax.random.normal(second, (PANELS, NB, NB), jnp.float32) * (0.6 / NB ** 0.5)
    below = jnp.clip(below, -0.5, 0.5)
    row_index = jnp.arange(NB)[:, None]
    col_index = jnp.arange(NB)[None, :]
    lower = jnp.where(row_index > col_index, below, 0.0)
    eye = (row_index == col_index).astype(jnp.float32)
    return lower + diagonal[:, :, None] * eye


def level_of(rng, extent, shards, low, largest):
    gain, own = 1.0, jax.random.fold_in(rng, 6)
    for axis_at, shards_of in shards:
        steps = jnp.exp(jax.random.uniform(jax.random.fold_in(own, axis_at), (shards_of,), jnp.float32, low / len(shards), largest / len(shards)))
        gain = gain * jnp.repeat(steps, extent[axis_at] // shards_of).reshape([-1 if axis == axis_at else 1 for axis in range(len(extent))])
    return gain


def centred(rng, dims, scale, reach, pieces=(), held_as=jnp.bfloat16):
    level = level_of(rng, dims, pieces, -0.22, 0.18) if pieces else 1.0
    entries = jax.random.normal(rng, dims, jnp.float32) * scale * level
    return jnp.minimum(jnp.maximum(entries, -reach), reach).astype(held_as)


def setup_inputs(seed: int = 0) -> dict:
    arg_keys = jax.random.split(jax.random.key(seed), 4)
    return {
        "right_side": centred(arg_keys[0], (ROWS, RHS), 1.0, 8.0, ((0, 8), (1, 64)), jnp.float32),
        "factor_panels": centred(arg_keys[1], (PANELS, NB, ROWS), (PANELS * NB) ** -0.5, 0.1875, ((1, 64), (2, 8)), jnp.float32),
        "inverses": draw_inverses(jax.random.fold_in(arg_keys[3], 71), 0),
    }


def solve_columns(columns, factor_panels, inverses):
    blocks_dev = ROW_DEV // NB
    stored_block = jnp.arange(ROWS, dtype=jnp.int32) // NB
    rank = (stored_block % blocks_dev) * N_ROW + stored_block // blocks_dev
    work = columns
    for panel in range(PANELS):
        stored = (panel % N_ROW) * blocks_dev + panel // N_ROW
        current = work[stored * NB:(stored + 1) * NB]
        answer = jnp.dot(inverses[panel], current, precision=lax.Precision.HIGHEST, preferred_element_type=jnp.float32)
        work = work.at[stored * NB:(stored + 1) * NB].set(answer)
        update = lax.dot_general(factor_panels[panel], answer, (((0,), (0,)), ((), ())), precision=lax.Precision.HIGHEST, preferred_element_type=jnp.float32)
        work = work - jnp.where((rank > panel)[:, None], update, jnp.zeros_like(update))
    return work


def reference(right_side, factor_panels, inverses):
    width = RHS_DEV
    stacked = right_side.reshape(ROWS, RHS // width, width).transpose(1, 0, 2)
    result = lax.map(lambda columns: solve_columns(columns, factor_panels, inverses), stacked)
    return result.transpose(1, 0, 2).reshape(ROWS, RHS)
```

```python
import jax
import jax.numpy as jnp
from jax import lax
from jax.experimental import pallas as pl
from jax.experimental.pallas import tpu as pltpu
from jax.sharding import PartitionSpec as P

MESH = pl.DeviceIdType.MESH
NZ = 16
PANELS = 4
OWNERS = 4
NB = 256
PAIRS = 6
BF16 = jnp.bfloat16
F32 = jnp.float32


def pair(m, k):
    return k * (k - 1) // 2 + m


def split(value):
    high = value.astype(BF16)
    low = (value - high.astype(F32)).astype(BF16)
    return high, low


def dot3(a, b, dims):
    def one(p, q):
        return lax.dot_general(p, q, (dims, ((), ())), preferred_element_type=F32)

    return one(a[0], b[0]) + (one(a[0], b[1]) + one(a[1], b[0]))


def kernel(
    rs_hbm, fac, inv, out_hbm,
    big, small, bvec, rs, xhi, xlo,
    ring_s, ring_r, x_s, x_r, sib_s, sibx_s, sib_ra, sib_rb,
    ch_s, ch_r, b_s, b_r, loc_s, out_s,
):
    row = lax.axis_index("row")
    col = lax.axis_index("col")
    xl, y = row // 4, row % 4
    xh, z, q = col // 32, (col // 2) % NZ, col % 2

    def at(row_to, xh_to, z_to, q_to):
        return (row_to, (xh_to * NZ + z_to) * 2 + q_to)

    up, down = at(row, xh, (z + 1) % NZ, q), at(row, xh, (z + NZ - 1) % NZ, q)
    towards = (up, down)
    sibling = at(row, xh, z, 1 - q)
    peer = at(row, 1 - xh, z, q)
    others = [at((row + i % 8) % 8, (xh + i // 8) % 2, z, q) for i in range(1, 16)]

    load_rs = pltpu.make_async_copy(rs_hbm, rs, loc_s.at[0])
    load_rs.start()
    own_big = pltpu.make_async_copy(fac, big.at[q, xh, z], loc_s.at[1])
    own_big.start()
    own_inv = pltpu.make_async_copy(inv, small.at[q, z, xh, pl.ds(0, PANELS)], loc_s.at[2])
    own_inv.start()

    barrier = pltpu.get_barrier_semaphore()
    greet = [up, down, sibling] + others
    for device in greet:
        pl.semaphore_signal(barrier, inc=1, device_id=device, device_id_type=MESH)
    pl.semaphore_wait(barrier, len(greet))

    def remote(src, dst, send, recv, device):
        return pltpu.make_async_remote_copy(
            src_ref=src, dst_ref=dst, send_sem=send, recv_sem=recv,
            device_id=device, device_id_type=MESH,
        )

    def chunk(origin, c):
        if c < 2:
            return small.at[q, origin, c]
        return big.at[q, xh, origin, pl.ds(2 * (c - 2), 2)]

    def ring(step, d, c):
        origin = (z + NZ - (step - 1)) % NZ if d == 0 else (z + step - 1) % NZ
        ref = chunk(origin, c)
        return remote(ref, ref, ring_s.at[d, step - 1, c], ring_r.at[d, step - 1, c], towards[d])

    def arrival(step, d, c):
        origin = (z + NZ - step) % NZ if d == 0 else (z + step) % NZ
        ref = chunk(origin, c)
        return origin, remote(
            ref, ref, ring_s.at[d, step - 1, c], ring_r.at[d, step - 1, c], towards[d]
        )

    def to_sibling(origin, slot, d, c):
        ref = chunk(origin, c)
        recv = sib_ra if c < 2 else sib_rb
        return remote(ref, ref, sib_s.at[d, slot, c], recv.at[0], sibling)

    def to_peer(origin, slot, d, c):
        ref = chunk(origin, c)
        return remote(ref, ref, x_s.at[d, slot, c - 2], x_r.at[d, slot], peer)

    def from_peer(origin, slot, d):
        ref = big.at[q, 1 - xh, origin]
        return remote(ref, ref, sibx_s.at[d, slot], x_r.at[d, slot], peer)

    def from_peer_half(origin, slot, d, c):
        ref = big.at[q, 1 - xh, origin, pl.ds(2 * (c - 2), 2)]
        return remote(ref, ref, sibx_s.at[d, slot], x_r.at[d, slot], peer)

    def peer_to_sibling(origin, slot, d):
        ref = big.at[q, 1 - xh, origin]
        return remote(ref, ref, sibx_s.at[d, slot], sib_rb.at[0], sibling)

    for k in (1, 2, 3):

        @pl.when(row == k)
        def _(k=k):
            place = pl.ds(PANELS + pair(0, k), k)
            src = fac.at[pl.ds(0, k), :, pl.ds(0, NB)]
            dst = small.at[q, z, xh, place]
            for i, device in enumerate(others):
                remote(src, dst, ch_s.at[i], ch_r.at[k - 1, xh], device).start()
            pltpu.make_async_copy(src, dst, ch_r.at[k - 1, xh]).start()

    inv_out = remote(
        inv, small.at[q, z, xh, pl.ds(0, PANELS)], ch_s.at[15], ch_r.at[3, 0], peer
    )
    inv_out.start()

    own_big.wait()
    for c in (2, 3):
        for d in (0, 1):
            ring(1, d, c).start()
        to_peer(z, 0, 0, c).start()
        to_sibling(z, 0, 0, c).start()

    head = pl.ds(0, NB)
    for k in range(OWNERS):

        @pl.when(row == k)
        def _(k=k):
            for i, device in enumerate(
                [at((k + 1) % 4, xh, z, q), at((k + 3) % 4, xh, z, q), at((k + 2) % 4, xh, z, q), at(k + 4, xh, z, q)]
            ):
                remote(rs_hbm.at[head], bvec.at[k], b_s.at[i], b_r.at[k], device).start()
            pltpu.make_async_copy(rs_hbm.at[head], bvec.at[k], b_r.at[k]).start()

    own_inv.wait()
    inv_in = small.at[q, z, 1 - xh, pl.ds(0, PANELS)]
    remote(inv, inv_in, ch_s.at[15], ch_r.at[3, 0], peer).wait_recv()
    for k in (1, 2, 3):
        for half in (0, 1):
            ref = small.at[q, z, half, pl.ds(PANELS + pair(0, k), k)]
            pltpu.make_async_copy(ref, ref, ch_r.at[k - 1, half]).wait()
    for c in (0, 1):
        for d in (0, 1):
            ring(1, d, c).start()
        to_sibling(z, 0, 0, c).start()

    def forward_b():
        for k in range(OWNERS):

            @pl.when(row == OWNERS + k)
            def _(k=k):
                pltpu.make_async_copy(rs_hbm.at[head], bvec.at[k], b_r.at[k]).wait()
                for i, device in enumerate(
                    [at(4 + (k + 1) % 4, xh, z, q), at(4 + (k + 3) % 4, xh, z, q), at(4 + (k + 2) % 4, xh, z, q)]
                ):
                    remote(bvec.at[k], bvec.at[k], b_s.at[i], b_r.at[k], device).start()

    def peer_arrivals(step):
        for d in (0, 1):
            origin = (z + NZ - step) % NZ if d == 0 else (z + step) % NZ
            from_peer(origin, step, d).wait_recv()
            peer_to_sibling(origin, step, d).start()

    def take(step, d, c, send):
        origin, copy = arrival(step, d, c)
        copy.wait_recv()
        if send:
            ring(step + 1, d, c).start()
        if c >= 2:
            to_peer(origin, step, d, c).start()
        to_sibling(origin, step, d, c).start()

    for c in (2, 3, 0, 1):
        for d in (0, 1):
            take(1, d, c, True)
    forward_b()
    from_peer(z, 0, 0).wait_recv()
    peer_to_sibling(z, 0, 0).start()

    def body(step, carry):
        for c in (0, 1, 2, 3):
            for d in (0, 1):
                take(step, d, c, True)
        peer_arrivals(step - 1)
        return carry

    lax.fori_loop(2, 7, body, 0)
    for c in (0, 1, 2, 3):
        for d in (0, 1):
            take(7, d, c, c % 2 == d)
    peer_arrivals(6)
    for c in (0, 1, 2, 3):
        take(8, c % 2, c, False)
    peer_arrivals(7)

    sib_small = small.at[1 - q]
    pltpu.make_async_copy(sib_small, sib_small, sib_ra.at[0]).wait()

    def square(index):
        halves = [
            jnp.concatenate([small[0, :, half, index], small[1, :, half, index]], axis=1).reshape(NB // 2, NB)
            for half in (0, 1)
        ]
        return jnp.concatenate(halves, axis=0)

    solved = []
    for k in range(PANELS):
        @pl.when(row != OWNERS + k)
        def _(k=k):
            pltpu.make_async_copy(rs_hbm.at[head], bvec.at[k], b_r.at[k]).wait()

        work = bvec[k]
        for m in range(k):
            work = work - dot3(split(square(PANELS + pair(m, k))), solved[m], ((0,), (0,)))
        answer = dot3(split(square(k)), split(work), ((1,), (0,)))

        if k == 0:
            load_rs.wait()

        @pl.when(row == k)
        def _(answer=answer):
            rs[head, :] = answer

        high, low = split(answer)
        solved.append((high, low))
        xhi[k] = high
        xlo[k] = low
        if k == 1:
            for c in (2, 3):
                origin = (z + NZ // 2) % NZ
                d = c % 2
                from_peer_half(origin, 8, d, c).wait_recv()
            peer_to_sibling((z + NZ // 2) % NZ, 8, 0).start()

    sib_big = big.at[1 - q]
    pltpu.make_async_copy(sib_big, sib_big, sib_rb.at[0]).wait()

    def update(block):
        lanes = pl.ds(pl.multiple_of(block * NB, NB), NB)
        total = jnp.zeros((NB, NB), F32)
        for k in range(PANELS):
            for half in (0, 1):
                factor = jnp.concatenate(
                    [big[0, half, :, k, :, lanes], big[1, half, :, k, :, lanes]], axis=1
                ).reshape(NB // 2, NB)
                rows_k = pl.ds(half * (NB // 2), NB // 2)
                x = (xhi[k, rows_k, :], xlo[k, rows_k, :])
                total = total + dot3(split(factor), x, ((0,), (0,)))
        rows = pl.ds(pl.multiple_of(block * NB, NB), NB)
        rs[rows, :] = rs[rows, :] - total

    def store(block):
        rows = pl.ds(pl.multiple_of(block * NB, NB), NB)
        return pltpu.make_async_copy(rs.at[rows], out_hbm.at[rows], out_s.at[block])

    @pl.when(row >= OWNERS)
    def _():
        update(0)

    store(0).start()

    def blocks(block, carry):
        update(block)
        store(block).start()
        return carry

    lax.fori_loop(1, 4, blocks, 0)

    for c in (2, 3):
        to_peer(z, 0, 0, c).wait_send()
    for c in range(4):
        to_sibling(z, 0, 0, c).wait_send()
    peer_to_sibling(z, 0, 0).wait_send()
    inv_out.wait_send()

    def drain(step, carry):
        for d in (0, 1):
            for c in range(4):
                ring(step, d, c).wait_send()
                to_sibling(z, step, d, c).wait_send()
                if c >= 2:
                    to_peer(z, step, d, c).wait_send()
            peer_to_sibling(z, step, d).wait_send()
        return carry

    lax.fori_loop(1, 8, drain, 0)
    for c in range(4):
        d = c % 2
        ring(8, d, c).wait_send()
        to_sibling(z, 8, d, c).wait_send()
        if c >= 2:
            to_peer(z, 8, d, c).wait_send()
    peer_to_sibling(z, 8, 0).wait_send()

    for k in (1, 2, 3):

        @pl.when(row == k)
        def _(k=k):
            src = fac.at[pl.ds(0, k), :, pl.ds(0, NB)]
            dst = small.at[q, z, xh, pl.ds(PANELS + pair(0, k), k)]
            for i, device in enumerate(others):
                remote(src, dst, ch_s.at[i], ch_r.at[k - 1, xh], device).wait_send()

    @pl.when(row < OWNERS)
    def _():
        for i in range(4):
            remote(rs_hbm.at[head], bvec.at[0], b_s.at[i], b_r.at[0], peer).wait_send()

    @pl.when(row >= OWNERS)
    def _():
        for i in range(3):
            remote(bvec.at[0], bvec.at[0], b_s.at[i], b_r.at[0], peer).wait_send()

    def finish(block, carry):
        store(block).wait()
        return carry

    lax.fori_loop(0, 4, finish, 0)


def per_device(right_side, factor_panels, inverses):
    rows, columns = right_side.shape
    dma = pltpu.SemaphoreType.DMA
    return pl.pallas_call(
        kernel,
        name="solve",
        out_shape=jax.ShapeDtypeStruct((rows, columns), F32),
        in_specs=[
            pl.BlockSpec(memory_space=pl.ANY),
            pl.BlockSpec(memory_space=pltpu.VMEM),
            pl.BlockSpec(memory_space=pltpu.VMEM),
        ],
        out_specs=pl.BlockSpec(memory_space=pl.ANY),
        scratch_shapes=[
            pltpu.VMEM((2, 2, NZ, PANELS, 4, rows), F32),
            pltpu.VMEM((2, NZ, 2, PANELS + PAIRS, 4, NB), F32),
            pltpu.VMEM((OWNERS, NB, columns), F32),
            pltpu.VMEM((rows, columns), F32),
            pltpu.VMEM((PANELS, NB, columns), BF16),
            pltpu.VMEM((PANELS, NB, columns), BF16),
            dma((2, 8, 4)),
            dma((2, 8, 4)),
            dma((2, 9, 2)),
            dma((2, 9)),
            dma((2, 9, 4)),
            dma((2, 9)),
            dma((1,)),
            dma((1,)),
            dma((16,)),
            dma((4, 2)),
            dma((4,)),
            dma((4,)),
            dma((3,)),
            dma((4,)),
        ],
        compiler_params=pltpu.CompilerParams(
            collective_id=0, has_side_effects=True, vmem_limit_bytes=48 << 20
        ),
        cost_estimate=pl.CostEstimate(flops=1 << 31, bytes_accessed=8 << 20, transcendentals=0),
    )(right_side, factor_panels, inverses)


def solution(mesh):
    in_specs = (P("row", "col"), P(None, "col", "row"), P(None, "col", None))
    return jax.shard_map(
        per_device, mesh=mesh, in_specs=in_specs, out_specs=P("row", "col"), check_vma=False
    )
```

```python
import jax
import jax.numpy as jnp
from jax import lax
from jax.experimental import pallas as pl
from jax.experimental.pallas import tpu as pltpu
from jax.sharding import PartitionSpec as P

MESH = pl.DeviceIdType.MESH
NZ = 16
PANELS = 4
OWNERS = 4
NB = 256
HALF = 128
CHUNKS = ((0, 2), (2, 2))
EXTRA = len(CHUNKS)
SLOTS = 5
BF16 = jnp.bfloat16
F32 = jnp.float32

INVERSE = {0: (0, 2), 1: (0, 3), 2: (0, 4), 3: (1, 4)}
BLOCK = {(0, 2): (0, 0), (1, 2): (0, 1), (0, 1): (1, 0), (0, 3): (1, 1), (1, 3): (1, 2), (2, 3): (1, 3)}


RING, RING_X, TREE, Y, X, PANEL, SIB, SIB_X, SIB_SMALL, SIB_PEER = range(10)


def split(value):
    high = value.astype(BF16)
    low = (value - high.astype(F32)).astype(BF16)
    return high, low


def dot3(a, b, dims):
    def one(p, q):
        return lax.dot_general(p, q, (dims, ((), ())), preferred_element_type=F32)

    return one(a[0], b[0]) + (one(a[0], b[1]) + one(a[1], b[0]))


def kernel(
    rs_hbm, fac, inv, out,
    big, small, bvec, xhi, xlo, ahi, alo,
    send, ring_r, tree_r, y_r, x_r, p_r, sib_r,
    ch_s, ch_r, b_s, b_r, loc_s,
):
    row = lax.axis_index("row")
    col = lax.axis_index("col")
    y, par = row % 4, row % 2
    xh, z, q = col // 32, (col // 2) % NZ, col % 2

    def at(row_to, xh_to, z_to, q_to):
        return (row_to, (xh_to * NZ + z_to) * 2 + q_to)

    def along_z(hop):
        return at(row, xh, (z + NZ + hop) % NZ, q)

    def along_y(hop):
        return at((row // 4) * 4 + (y + 4 + hop) % 4, xh, z, q)

    sibling = at(row, xh, z, 1 - q)
    peer = at(row, 1 - xh, z, q)
    others = [at((row + i % 8) % 8, (xh + i // 8) % 2, z, q) for i in range(1, 16)]
    alike = [at((row + 2 * (i % 4)) % 8, (xh + i // 4) % 2, z, q) for i in range(1, 8)]

    own_big = pltpu.make_async_copy(fac, big.at[q, xh, z], loc_s.at[1])
    own_big.start()
    load_rs = pltpu.make_async_copy(rs_hbm, out, loc_s.at[0])
    load_rs.start()

    barrier = pltpu.get_barrier_semaphore()
    greet = [along_z(hop) for hop in (1, -1, 2, -2)] + [sibling] + others
    for device in greet:
        pl.semaphore_signal(barrier, inc=1, device_id=device, device_id_type=MESH)
    pl.semaphore_wait(barrier, len(greet))

    def remote(src, dst, send, recv, device):
        return pltpu.make_async_remote_copy(
            src_ref=src, dst_ref=dst, send_sem=send, recv_sem=recv,
            device_id=device, device_id_type=MESH,
        )

    def origin_of(distance, d):
        return (z + NZ - distance) % NZ if d == 0 else (z + distance) % NZ

    def chunk(origin, c):
        if c == EXTRA:
            return big.at[q, 1 - xh, origin, pl.ds(0, 1)]
        return big.at[q, xh, origin, pl.ds(CHUNKS[c][0], CHUNKS[c][1])]

    def ring(step, d, c):
        ref = chunk(origin_of(step - 1, d), c)
        return remote(
            ref, ref, send.at[RING if c < EXTRA else RING_X], ring_r.at[d, step - 1, c], along_z(1 if d == 0 else -1)
        )

    def arrival(step, d, c):
        ref = chunk(origin_of(step, d), c)
        return remote(
            ref, ref, send.at[RING if c < EXTRA else RING_X], ring_r.at[d, step - 1, c], along_z(1 if d == 0 else -1)
        )

    def crosses(c):
        return c < EXTRA and sum(CHUNKS[c]) > 1

    def to_sibling(origin, slot, d, c):
        ref = chunk(origin, c)
        return remote(ref, ref, send.at[SIB if c < EXTRA else SIB_X], sib_r.at[2 if c == EXTRA else 1], sibling)

    def to_peer(origin, slot, d, c):
        first = max(CHUNKS[c][0], 1)
        ref = big.at[q, xh, origin, pl.ds(first, sum(CHUNKS[c]) - first)]
        return remote(ref, ref, send.at[X], x_r.at[d, slot], peer)

    def peer_part(origin, part):
        return big.at[q, 1 - xh, origin, part]

    def from_peer(origin, slot, d, part):
        ref = peer_part(origin, part)
        return remote(ref, ref, send.at[SIB_PEER], x_r.at[d, slot], peer)

    def peer_to_sibling(origin, slot, d, part):
        ref = peer_part(origin, part)
        return remote(ref, ref, send.at[SIB_PEER], sib_r.at[3], sibling)

    REST, ONE, TWO = pl.ds(1, 3), pl.ds(1, 1), pl.ds(2, 2)

    def last_leaves(d, c):
        return (d == 1) == (c < EXTRA and CHUNKS[c][0] >= 2)

    LAST = [(d, c) for c in range(EXTRA + 1) for d in (0, 1) if last_leaves(d, c)]

    def take_big(step, d, c, send):
        arrival(step, d, c).wait_recv()
        if send:
            ring(step + 1, d, c).start()
        origin = origin_of(step, d)
        if crosses(c):
            to_peer(origin, step, d, c).start()
        to_sibling(origin, step, d, c).start()

    def peer_arrivals(step):
        for d in (0, 1):
            origin = origin_of(step, d)
            from_peer(origin, step, d, REST).wait_recv()
            peer_to_sibling(origin, step, d, REST).start()

    def small_part(parity, origin, h):
        return small.at[q, parity, origin, h]

    def tree(held, hop, d, h):
        ref = small_part(par, origin_of(held, d), h)
        to = held + hop - 1
        return remote(ref, ref, send.at[TREE], tree_r.at[d, to, h], along_z(hop if d == 0 else -hop))

    def small_arrival(distance, d, h):
        ref = small_part(par, origin_of(distance, d), h)
        return remote(ref, ref, send.at[TREE], tree_r.at[d, distance - 1, h], along_z(1))

    def small_to_y(distance, d, h):
        ref = small_part(par, origin_of(distance, d), h)
        return remote(ref, ref, send.at[Y], y_r.at[d, distance, h], along_y(1 if h == 0 else -1))

    def small_to_sibling(distance, d, h):
        ref = small_part(par, origin_of(distance, d), h)
        return remote(ref, ref, send.at[SIB_SMALL], sib_r.at[0], sibling)

    def y_arrival(distance, d, h):
        ref = small_part(1 - par, origin_of(distance, d), h)
        return remote(ref, ref, send.at[Y], y_r.at[d, distance, h], sibling)

    def y_to_sibling(distance, d, h):
        ref = small_part(1 - par, origin_of(distance, d), h)
        return remote(ref, ref, send.at[SIB_SMALL], sib_r.at[0], sibling)

    def take_small(distance, even, last, d, h):
        small_arrival(distance, d, h).wait_recv()
        if even:
            if not last or h == d:
                tree(distance, 2, d, h).start()
            tree(distance, 1, d, h).start()
        small_to_y(distance, d, h).start()
        small_to_sibling(distance, d, h).start()

    def take_y(distance, d, h):
        y_arrival(distance, d, h).wait_recv()
        y_to_sibling(distance, d, h).start()

    def chain(k):
        parity, slot = BLOCK[(0, k)]
        src = fac.at[pl.ds(0, k), :, pl.ds(0, NB)]
        dst = small.at[q, parity, z, xh, pl.ds(slot, k)]
        return src, dst

    def inverse_part(parity, h):
        src = inv.at[pl.ds(0, 3)] if parity == 0 else inv.at[pl.ds(3, 1)]
        dst = small.at[q, parity, z, h, pl.ds(2, 3) if parity == 0 else pl.ds(4, 1)]
        return src, dst

    for k in (1, 2, 3):

        @pl.when(row == k)
        def _(k=k):
            src, dst = chain(k)
            for i, device in enumerate(alike):
                remote(src, dst, ch_s.at[i], ch_r.at[k - 1, xh], device).start()
            pltpu.make_async_copy(src, dst, ch_r.at[k - 1, xh]).start()

    for parity in (0, 1):

        @pl.when(par == parity)
        def _(parity=parity):
            src, dst = inverse_part(parity, xh)
            remote(src, dst, ch_s.at[7], ch_r.at[3, 0], peer).start()
            pltpu.make_async_copy(src, dst, ch_r.at[3, 1]).start()

    def b_half(ref, part):
        return ref.at[pl.ds(part * HALF, HALF)]

    def b_cross(k, part):
        return remote(
            b_half(rs_hbm, part), b_half(bvec.at[k], part), b_s.at[3, part], b_r.at[k, part], at(k + 4, xh, z, q)
        )

    for k in range(OWNERS):

        @pl.when(row == k)
        def _(k=k):
            for part in (0, 1):
                b_cross(k, part).start()

    own_big.wait()
    own_panel = big.at[q, xh, z, pl.ds(0, 1)]
    panel_out = remote(own_panel, own_panel, send.at[PANEL], p_r.at[0], peer)
    panel_out.start()
    for c in range(EXTRA):
        for d in (0, 1):
            ring(1, d, c).start()
    for c in range(EXTRA):
        if crosses(c):
            to_peer(z, 0, 0, c).start()
        to_sibling(z, 0, 0, c).start()

    for k in range(OWNERS):

        @pl.when(row == k)
        def _(k=k):
            for part in (0, 1):
                for i, hop in enumerate((1, -1, 2)):
                    remote(
                        b_half(rs_hbm, part), b_half(bvec.at[k], part), b_s.at[i, part], b_r.at[k, part], along_y(hop)
                    ).start()
                pltpu.make_async_copy(
                    b_half(rs_hbm, part), b_half(bvec.at[k], part), b_r.at[k, part]
                ).start()

    def b_wait(k, part):
        pltpu.make_async_copy(b_half(rs_hbm, part), b_half(bvec.at[k], part), b_r.at[k, part]).wait()

    def forward_b(part):
        for k in range(OWNERS):

            @pl.when(row == OWNERS + k)
            def _(k=k):
                b_wait(k, part)
                ref = b_half(bvec.at[k], part)
                for i, hop in enumerate((1, -1, 2)):
                    remote(ref, ref, b_s.at[i, part], b_r.at[k, part], along_y(hop)).start()

    peer_panel = big.at[q, 1 - xh, z, pl.ds(0, 1)]
    remote(peer_panel, peer_panel, send.at[PANEL], p_r.at[0], peer).wait_recv()
    for d in (0, 1):
        ring(1, d, EXTRA).start()
    to_sibling(z, 0, 0, EXTRA).start()

    for c in range(EXTRA):
        for d in (0, 1):
            take_big(1, d, c, True)

    for parity in (0, 1):

        @pl.when(par == parity)
        def _(parity=parity):
            for sem, h in ((ch_r.at[3, 1], xh), (ch_r.at[3, 0], 1 - xh)):
                src, dst = inverse_part(parity, h)
                pltpu.make_async_copy(src, dst, sem).wait()
            for k in (2,) if parity == 0 else (1, 3):
                for h in (0, 1):
                    ref = small.at[q, parity, z, h, pl.ds(BLOCK[(0, k)][1], k)]
                    pltpu.make_async_copy(ref, ref, ch_r.at[k - 1, h]).wait()

    for h in (0, 1):
        for d in (0, 1):
            tree(0, 2, d, h).start()
            tree(0, 1, d, h).start()
        small_to_y(0, 0, h).start()
        small_to_sibling(0, 0, h).start()

    for d in (0, 1):
        take_big(1, d, EXTRA, True)
    from_peer(z, 0, 0, REST).wait_recv()
    peer_to_sibling(z, 0, 0, REST).start()

    def big_step(step):
        for c in range(EXTRA + 1):
            for d in (0, 1):
                take_big(step, d, c, True)
        if step > 2:
            peer_arrivals(step - 2)

    big_step(2)
    forward_b(0)

    def steps(j, carry):
        for h in (0, 1):
            for d in (0, 1):
                small_arrival(2 * j, d, h).wait_recv()
                if h == d:
                    tree(2 * j, 2, d, h).start()
                else:

                    @pl.when(j < 3)
                    def _(d=d, h=h):
                        tree(2 * j, 2, d, h).start()

                tree(2 * j, 1, d, h).start()
                small_to_y(2 * j, d, h).start()
                small_to_sibling(2 * j, d, h).start()
        for h in (0, 1):
            for d in (0, 1):
                take_small(2 * j - 1, False, False, d, h)

        @pl.when(j == 1)
        def _():
            forward_b(1)
            for h in (0, 1):
                take_y(0, 0, h)

        @pl.when(j > 1)
        def _():
            for h in (0, 1):
                for d in (0, 1):
                    take_y(2 * j - 3, d, h)
                    take_y(2 * j - 2, d, h)

        for c in range(EXTRA + 1):
            for d in (0, 1):
                take_big(j + 2, d, c, True)
        peer_arrivals(j + 0)
        return carry

    lax.fori_loop(1, 4, steps, 0)
    for h in (0, 1):
        take_small(8, False, False, h, h)
    for h in (0, 1):
        for d in (0, 1):
            take_small(7, False, False, d, h)
    for h in (0, 1):
        for d in (0, 1):
            take_y(5, d, h)
            take_y(6, d, h)
    for c in range(EXTRA + 1):
        for d in (0, 1):
            take_big(6, d, c, True)
    peer_arrivals(4)
    for h in (0, 1):
        take_y(8, h, h)
        for d in (0, 1):
            take_y(7, d, h)

    for c in range(EXTRA + 1):
        for d in (0, 1):
            take_big(7, d, c, last_leaves(d, c))
    peer_arrivals(5)

    sib_small = small.at[1 - q]
    pltpu.make_async_copy(sib_small, sib_small, sib_r.at[0]).wait()

    def prepare(place, carry):
        parity, slot = place // SLOTS, place % SLOTS
        for half in (0, 1):
            value = jnp.concatenate(
                [small[0, parity, :, half, slot], small[1, parity, :, half, slot]], axis=1
            ).reshape(HALF, NB)
            ahi[place, pl.ds(half * HALF, HALF), :], alo[place, pl.ds(half * HALF, HALF), :] = split(value)
        return carry

    lax.fori_loop(0, 2 * SLOTS, prepare, 0)
    load_rs.wait()

    def solve(k, carry):
        @pl.when(row != OWNERS + k)
        def _():
            for part in (0, 1):
                b_wait(k, part)

        def reduce(m, work):
            place = m + (k % 2) * (5 + k // 2)
            x = tuple(ref[m].reshape(NB, NB) for ref in (xhi, xlo))
            return work - dot3((ahi[place], alo[place]), x, ((0,), (0,)))

        work = lax.fori_loop(0, k, reduce, bvec[k])
        place = 2 + k + 4 * (k // 3)
        answer = dot3((ahi[place], alo[place]), split(work), ((1,), (0,)))

        @pl.when(row == k)
        def _():
            out[pl.ds(0, NB), :] = answer

        high, low = split(answer)
        xhi[k] = high.reshape(2, HALF, NB)
        xlo[k] = low.reshape(2, HALF, NB)

        @pl.when(k == 0)
        def _():
            for d, c in LAST:
                take_big(8, d, c, False)
            peer_arrivals(6)

        @pl.when(k == 2)
        def _():
            peer_arrivals(7)

        return carry

    lax.fori_loop(0, PANELS, solve, 0)
    for d, part in ((0, ONE), (1, TWO)):
        origin = origin_of(8, d)
        from_peer(origin, 8, d, part).wait_recv()
        peer_to_sibling(origin, 8, d, part).start()

    def update(block, parts):
        lanes = pl.ds(pl.multiple_of(block * NB, NB), NB)

        def factor(half, k):
            return jnp.concatenate(
                [big[0, half, :, k, :, lanes], big[1, half, :, k, :, lanes]], axis=1
            ).reshape(HALF, NB)

        total = None
        for group in parts:
            f = jnp.concatenate([factor(half, k) for half, k in group], axis=0)
            x = tuple(
                jnp.concatenate([ref[k, half] for half, k in group], axis=0) for ref in (xhi, xlo)
            )
            term = dot3(split(f), x, ((0,), (0,)))
            total = term if total is None else total + term
        rows = pl.ds(pl.multiple_of(block * NB, NB), NB)
        out[rows, :] = out[rows, :] - total

    def all_blocks(parts):
        def blocks(block, carry):
            update(block, parts)
            return carry

        lax.fori_loop(1 - row // OWNERS, 4, blocks, 0)

    own_half = big.at[1 - q, xh]
    pltpu.make_async_copy(own_half, own_half, sib_r.at[1]).wait()
    one_panel = big.at[1 - q, 1 - xh, :, pl.ds(0, 1)]
    pltpu.make_async_copy(one_panel, one_panel, sib_r.at[2]).wait()
    all_blocks((((xh, 0), (xh, 1)), ((xh, 2), (xh, 3)), ((1 - xh, 0),)))
    rest = big.at[1 - q, 1 - xh, :, REST]
    pltpu.make_async_copy(rest, rest, sib_r.at[3]).wait()
    all_blocks((((1 - xh, 1), (1 - xh, 2)), ((1 - xh, 3),)))

    def left(kind, ref):
        pltpu.make_async_copy(ref, ref, send.at[kind]).wait()

    most = pl.ds(0, NZ - 1)
    left(PANEL, own_panel)
    left(RING, big.at[q, xh, most])
    left(RING_X, big.at[q, 1 - xh, most, pl.ds(0, 1)])
    left(TREE, small.at[q, par, most])
    left(Y, small.at[q, par])
    left(X, big.at[q, xh, :, REST])
    left(SIB, big.at[q, xh])
    left(SIB_X, big.at[q, 1 - xh, :, pl.ds(0, 1)])
    left(SIB_SMALL, small.at[q])
    left(SIB_PEER, big.at[q, 1 - xh, :, REST])

    for k in (1, 2, 3):

        @pl.when(row == k)
        def _(k=k):
            src, dst = chain(k)
            for i, device in enumerate(alike):
                remote(src, dst, ch_s.at[i], ch_r.at[k - 1, xh], device).wait_send()

    for parity in (0, 1):

        @pl.when(par == parity)
        def _(parity=parity):
            src, dst = inverse_part(parity, xh)
            remote(src, dst, ch_s.at[7], ch_r.at[3, 0], peer).wait_send()

    for part in (0, 1):
        ref = b_half(bvec.at[0], part)
        for i in range(3):
            remote(ref, ref, b_s.at[i, part], b_r.at[0, part], peer).wait_send()

    @pl.when(row < OWNERS)
    def _():
        for part in (0, 1):
            b_cross(0, part).wait_send()


def per_device(right_side, factor_panels, inverses):
    rows, columns = right_side.shape
    dma = pltpu.SemaphoreType.DMA
    return pl.pallas_call(
        kernel,
        name="solve",
        out_shape=pltpu.VMEM((rows, columns), F32),
        in_specs=[pl.BlockSpec(memory_space=pltpu.HBM)] * 3,
        out_specs=pl.BlockSpec(memory_space=pltpu.VMEM),
        scratch_shapes=[
            pltpu.VMEM((2, 2, NZ, PANELS, 4, rows), F32),
            pltpu.VMEM((2, 2, NZ, 2, SLOTS, 4, NB), F32),
            pltpu.VMEM((OWNERS, NB, columns), F32),
            pltpu.VMEM((PANELS, 2, HALF, columns), BF16),
            pltpu.VMEM((PANELS, 2, HALF, columns), BF16),
            pltpu.VMEM((2 * SLOTS, NB, NB), BF16),
            pltpu.VMEM((2 * SLOTS, NB, NB), BF16),
            dma((10,)),
            dma((2, 8, EXTRA + 1)),
            dma((2, 8, 2)),
            dma((2, 9, 2)),
            dma((2, 9)),
            dma((1,)),
            dma((4,)),
            dma((8,)),
            dma((4, 2)),
            dma((4, 2)),
            dma((4, 2)),
            dma((2,)),
        ],
        compiler_params=pltpu.CompilerParams(
            collective_id=0, has_side_effects=True, vmem_limit_bytes=62 << 20
        ),
        cost_estimate=pl.CostEstimate(flops=1 << 31, bytes_accessed=8 << 20, transcendentals=0),
    )(right_side, factor_panels, inverses)


def solution(mesh):
    in_specs = (P("row", "col"), P(None, "col", "row"), P(None, "col", None))
    return jax.shard_map(
        per_device, mesh=mesh, in_specs=in_specs, out_specs=P("row", "col"), check_vma=False
    )
```

```python
import jax
import jax.numpy as jnp
from jax import lax
from jax.experimental import pallas as pl
from jax.experimental.pallas import tpu as pltpu
from jax.sharding import PartitionSpec as P

MESH = pl.DeviceIdType.MESH
NZ = 16
PANELS = 4
OWNERS = 4
NB = 256
HALF = 128
CHUNKS = ((0, 2), (2, 2))
SLOTS = 3
BF16 = jnp.bfloat16
F32 = jnp.float32

def block_place(m, k):
    return SLOTS * k + m


def inverse_place(k):
    return k + k // 3


RING, TREE, Y, RELAY, X, SIB, SIB_SMALL, SIB_PEER = range(8)


def split(value):
    high = value.astype(BF16)
    low = (value - high.astype(F32)).astype(BF16)
    return high, low


def dot3(a, b, dims):
    def one(p, q):
        return lax.dot_general(p, q, (dims, ((), ())), preferred_element_type=F32)

    return one(a[0], b[0]) + (one(a[0], b[1]) + one(a[1], b[0]))


def kernel(
    rs_hbm, fac, inv, out,
    big, small, bvec, xhi, xlo, ahi, alo,
    send, ring_r, tree_r, y_r, x_r, sib_r,
    ch_s, ch_r, b_s, b_r, loc_s,
):
    row = lax.axis_index("row")
    col = lax.axis_index("col")
    y = row % 4
    xh, z, q = col // 32, (col // 2) % NZ, col % 2

    def at(row_to, xh_to, z_to, q_to):
        return (row_to, (xh_to * NZ + z_to) * 2 + q_to)

    def along_z(hop):
        return at(row, xh, (z + NZ + hop) % NZ, q)

    def along_y(hop):
        return at((row // 4) * 4 + (y + 4 + hop) % 4, xh, z, q)

    sibling = at(row, xh, z, 1 - q)
    peer = at(row, 1 - xh, z, q)
    alike = [at((row + 4 * (i % 2)) % 8, (xh + i // 2) % 2, z, q) for i in (1, 2, 3)]
    across_y = [along_y(1), along_y(-1)]
    before, after, over = (y + 3) % 4, (y + 1) % 4, (y + 2) % 4

    own_big = pltpu.make_async_copy(fac, big.at[q, xh, z], loc_s.at[1])
    own_big.start()
    load_rs = pltpu.make_async_copy(rs_hbm, out, loc_s.at[0])
    load_rs.start()

    barrier = pltpu.get_barrier_semaphore()
    greet = [along_z(hop) for hop in (1, -1, 2, -2)] + [sibling] + alike + across_y
    for device in greet:
        pl.semaphore_signal(barrier, inc=1, device_id=device, device_id_type=MESH)
    pl.semaphore_wait(barrier, len(greet))

    def remote(src, dst, send, recv, device):
        return pltpu.make_async_remote_copy(
            src_ref=src, dst_ref=dst, send_sem=send, recv_sem=recv,
            device_id=device, device_id_type=MESH,
        )

    def origin_of(distance, d):
        return (z + NZ - distance) % NZ if d == 0 else (z + distance) % NZ

    def chunk(origin, c):
        return big.at[q, xh, origin, pl.ds(CHUNKS[c][0], CHUNKS[c][1])]

    def hop_to(hop, d):
        return along_z(hop if d == 0 else -hop)

    def grow(held, hop, d, c):
        ref = chunk(origin_of(held, d), c)
        return remote(ref, ref, send.at[RING], ring_r.at[d, held + hop - 1, c], hop_to(hop, d))

    def arrival(distance, d, c):
        ref = chunk(origin_of(distance, d), c)
        return remote(ref, ref, send.at[RING], ring_r.at[d, distance - 1, c], hop_to(1, d))

    def to_sibling(origin, slot, d, c):
        ref = chunk(origin, c)
        return remote(ref, ref, send.at[SIB], sib_r.at[1], sibling)

    def to_peer(origin, slot, d, c):
        ref = chunk(origin, c)
        return remote(ref, ref, send.at[X], x_r.at[d, slot], peer)

    def peer_part(origin, part):
        return big.at[q, 1 - xh, origin, part]

    def from_peer(origin, slot, d, part):
        ref = peer_part(origin, part)
        return remote(ref, ref, send.at[SIB_PEER], x_r.at[d, slot], peer)

    def peer_to_sibling(origin, slot, d, part):
        ref = peer_part(origin, part)
        return remote(ref, ref, send.at[SIB_PEER], sib_r.at[3], sibling)

    REST, ONE, TWO = pl.ds(0, 4), pl.ds(0, 2), pl.ds(2, 2)

    def last_leaves(d, c):
        return (d == 1) == (CHUNKS[c][0] >= 2)

    LAST = [(d, c) for c in range(len(CHUNKS)) for d in (0, 1) if last_leaves(d, c)]

    def hand_on(distance, d, c):
        origin = origin_of(distance, d)
        to_peer(origin, distance, d, c).start()
        to_sibling(origin, distance, d, c).start()

    def take_end(distance, d, c):
        arrival(distance, d, c).wait_recv()
        hand_on(distance, d, c)

    def peer_arrivals(step):
        for d in (0, 1):
            origin = origin_of(step, d)
            from_peer(origin, step, d, REST).wait_recv()
            peer_to_sibling(origin, step, d, REST).start()

    def small_part(quarter, origin, h):
        return small.at[q, quarter, origin, h]

    def tree(held, hop, d, h):
        ref = small_part(y, origin_of(held, d), h)
        to = held + hop - 1
        return remote(ref, ref, send.at[TREE], tree_r.at[d, to, h], along_z(hop if d == 0 else -hop))

    def small_arrival(distance, d, h):
        ref = small_part(y, origin_of(distance, d), h)
        return remote(ref, ref, send.at[TREE], tree_r.at[d, distance - 1, h], along_z(1))

    def small_to_y(distance, d, h, i):
        ref = small_part(y, origin_of(distance, d), h)
        return remote(ref, ref, send.at[Y], y_r.at[i, d, distance, h], across_y[i])

    def small_to_sibling(distance, d, h):
        ref = small_part(y, origin_of(distance, d), h)
        return remote(ref, ref, send.at[SIB_SMALL], sib_r.at[0], sibling)

    def y_arrival(distance, d, h, i):
        ref = small_part((before, after, over)[i], origin_of(distance, d), h)
        return remote(ref, ref, send.at[SIB_SMALL], y_r.at[i, d, distance, h], sibling)

    def y_to_sibling(distance, d, h, i):
        ref = small_part((before, after, over)[i], origin_of(distance, d), h)
        return remote(ref, ref, send.at[SIB_SMALL], sib_r.at[0], sibling)

    def relay(distance, d, h):
        ref = small_part((before, after)[h], origin_of(distance, d), h)
        return remote(ref, ref, send.at[RELAY], y_r.at[2, d, distance, h], across_y[h])

    def spread(distance, d, h):
        for i in (0, 1):
            small_to_y(distance, d, h, i).start()
        small_to_sibling(distance, d, h).start()

    def take_odd(distance, d, h):
        small_arrival(distance, d, h).wait_recv()
        spread(distance, d, h)

    def take_y(distance, d, h):
        for i in (0, 1):
            y_arrival(distance, d, h, i).wait_recv()
            if i == h:
                relay(distance, d, h).start()
            y_to_sibling(distance, d, h, i).start()

    def take_over(distance, d, h):
        y_arrival(distance, d, h, 2).wait_recv()
        y_to_sibling(distance, d, h, 2).start()

    def chain(k, h):
        return fac.at[pl.ds(0, k), :, pl.ds(0, NB)], small.at[q, k, z, h, pl.ds(0, k)]

    for k in (1, 2, 3):

        @pl.when(row == k)
        def _(k=k):
            src, dst = chain(k, xh)
            for i, device in enumerate(alike):
                remote(src, dst, ch_s.at[i], ch_r.at[xh], device).start()
            pltpu.make_async_copy(src, dst, ch_r.at[xh]).start()

    def inverse_part(quarter, h):
        src = inv.at[pl.ds(0, 3)] if quarter == 0 else inv.at[pl.ds(3, 1)]
        return src, small.at[q, quarter, z, h, pl.ds(0, 3) if quarter == 0 else pl.ds(1, 1)]

    for quarter in (0, 1):

        @pl.when(y == quarter)
        def _(quarter=quarter):
            src, dst = inverse_part(quarter, xh)
            remote(src, dst, ch_s.at[3], ch_r.at[2], peer).start()
            pltpu.make_async_copy(src, dst, ch_r.at[3]).start()

    @pl.when((y == 1) | (y == 2))
    def _():
        for h in (0, 1):
            small[q, y, z, h, 2] = jnp.zeros((4, NB), F32)

    def b_half(ref, part):
        return ref.at[pl.ds(part * HALF, HALF)]

    def b_cross(k, part):
        return remote(
            b_half(rs_hbm, part), b_half(bvec.at[k], part), b_s.at[3, part], b_r.at[k, part], at(k + 4, xh, z, q)
        )

    for k in range(OWNERS):

        @pl.when(row == k)
        def _(k=k):
            for part in (0, 1):
                b_cross(k, part).start()

    own_big.wait()
    for c in range(len(CHUNKS)):
        for d in (0, 1):
            grow(0, 2, d, c).start()
            grow(0, 1, d, c).start()
    for c in range(len(CHUNKS)):
        to_peer(z, 0, 0, c).start()
        to_sibling(z, 0, 0, c).start()

    for k in range(OWNERS):

        @pl.when(row == k)
        def _(k=k):
            for part in (0, 1):
                for i in (0, 1):
                    remote(
                        b_half(rs_hbm, part), b_half(bvec.at[k], part), b_s.at[i, part], b_r.at[k, part], across_y[i]
                    ).start()
                pltpu.make_async_copy(
                    b_half(rs_hbm, part), b_half(bvec.at[k], part), b_r.at[k, part]
                ).start()

    def b_wait(k, part):
        pltpu.make_async_copy(b_half(rs_hbm, part), b_half(bvec.at[k], part), b_r.at[k, part]).wait()

    def forward_b(part):
        for k in range(OWNERS):

            @pl.when(row == OWNERS + k)
            def _(k=k):
                b_wait(k, part)
                ref = b_half(bvec.at[k], part)
                for i in (0, 1):
                    remote(ref, ref, b_s.at[i, part], b_r.at[k, part], across_y[i]).start()

    def relay_b(part):
        k = (before, after)[part]
        b_wait(k, part)
        ref = b_half(bvec.at[k], part)
        remote(ref, ref, b_s.at[2, part], b_r.at[k, part], across_y[part]).start()

    for quarter in (0, 1):

        @pl.when(y == quarter)
        def _(quarter=quarter):
            for sem, h in ((ch_r.at[3], xh), (ch_r.at[2], 1 - xh)):
                src, dst = inverse_part(quarter, h)
                pltpu.make_async_copy(src, dst, sem).wait()

    for k in (1, 2, 3):

        @pl.when(y == k)
        def _(k=k):
            for h in (0, 1):
                src, dst = chain(k, h)
                pltpu.make_async_copy(src, dst, ch_r.at[h]).wait()

    for h in (0, 1):
        for d in (0, 1):
            tree(0, 2, d, h).start()
            tree(0, 1, d, h).start()
        spread(0, 0, h)

    def steps(j, carry):
        for c in range(len(CHUNKS)):
            for d in (0, 1):
                arrival(2 * j, d, c).wait_recv()
                if last_leaves(d, c):
                    grow(2 * j, 2, d, c).start()
                else:

                    @pl.when(j < 3)
                    def _(d=d, c=c):
                        grow(2 * j, 2, d, c).start()

                grow(2 * j, 1, d, c).start()
                hand_on(2 * j, d, c)
        for h in (0, 1):
            for d in (0, 1):
                small_arrival(2 * j, d, h).wait_recv()
                if h == d:
                    tree(2 * j, 2, d, h).start()
                else:

                    @pl.when(j < 3)
                    def _(d=d, h=h):
                        tree(2 * j, 2, d, h).start()

                tree(2 * j, 1, d, h).start()
                spread(2 * j, d, h)
        for h in (0, 1):
            for d in (0, 1):
                take_odd(2 * j - 1, d, h)

        for c in range(len(CHUNKS)):
            for d in (0, 1):
                take_end(2 * j - 1, d, c)

        @pl.when(j == 1)
        def _():
            from_peer(z, 0, 0, REST).wait_recv()
            peer_to_sibling(z, 0, 0, REST).start()
            forward_b(0)
            for h in (0, 1):
                take_y(0, 0, h)

        @pl.when(j > 1)
        def _():
            for h in (0, 1):
                for d in (0, 1):
                    take_y(2 * j - 3, d, h)
                    take_y(2 * j - 2, d, h)
            peer_arrivals(2 * j - 3)
            peer_arrivals(2 * j - 2)

        @pl.when(j == 2)
        def _():
            forward_b(1)
            for h in (0, 1):
                take_over(0, 0, h)

        @pl.when(j == 3)
        def _():
            for part in (0, 1):
                relay_b(part)
            for h in (0, 1):
                for d in (0, 1):
                    take_over(1, d, h)
                    take_over(2, d, h)

        return carry

    lax.fori_loop(1, 4, steps, 0)
    for d, c in LAST:
        take_end(8, d, c)
    for h in (0, 1):
        take_odd(8, h, h)
    for h in (0, 1):
        for d in (0, 1):
            take_odd(7, d, h)
    for c in range(len(CHUNKS)):
        for d in (0, 1):
            take_end(7, d, c)
    for h in (0, 1):
        for d in (0, 1):
            take_y(5, d, h)
            take_y(6, d, h)
            take_over(3, d, h)
            take_over(4, d, h)
    peer_arrivals(5)
    peer_arrivals(6)
    for h in (0, 1):
        take_y(8, h, h)
        for d in (0, 1):
            take_y(7, d, h)
            take_over(5, d, h)
            take_over(6, d, h)
    for h in (0, 1):
        take_over(8, h, h)
        for d in (0, 1):
            take_over(7, d, h)

    sib_small = small.at[1 - q]
    pltpu.make_async_copy(sib_small, sib_small, sib_r.at[0]).wait()

    @pl.when(row < OWNERS)
    def _():
        for part in (0, 1):
            b_wait(y, part)

    b_wait(before, 1)
    b_wait(after, 0)
    for part in (0, 1):
        b_wait(over, part)

    def prepare(place, carry):
        quarter, slot = place // SLOTS, place % SLOTS
        for half in (0, 1):
            value = jnp.concatenate(
                [small[0, quarter, :, half, slot], small[1, quarter, :, half, slot]], axis=1
            ).reshape(HALF, NB)
            ahi[place, pl.ds(half * HALF, HALF), :], alo[place, pl.ds(half * HALF, HALF), :] = split(value)
        return carry

    lax.fori_loop(0, 5, prepare, 0)
    lax.fori_loop(6, 8, prepare, 0)
    lax.fori_loop(9, 12, prepare, 0)
    load_rs.wait()

    work = [bvec[k] for k in range(PANELS)]
    for k in range(PANELS):
        place = inverse_place(k)
        answer = dot3((ahi[place], alo[place]), split(work[k]), ((1,), (0,)))
        x = split(answer)
        for m in range(k + 1, PANELS):
            place = block_place(k, m)
            work[m] = work[m] - dot3((ahi[place], alo[place]), x, ((0,), (0,)))

        @pl.when(row == k)
        def _(answer=answer):
            out[pl.ds(0, NB), :] = answer

        xhi[k] = x[0].reshape(2, HALF, NB)
        xlo[k] = x[1].reshape(2, HALF, NB)
        if k == 1:
            peer_arrivals(7)
    for d, part in ((0, ONE), (1, TWO)):
        origin = origin_of(8, d)
        from_peer(origin, 8, d, part).wait_recv()
        peer_to_sibling(origin, 8, d, part).start()

    def update(block, parts):
        lanes = pl.ds(pl.multiple_of(block * NB, NB), NB)

        def factor(half, k):
            return jnp.concatenate(
                [big[0, half, :, k, :, lanes], big[1, half, :, k, :, lanes]], axis=1
            ).reshape(HALF, NB)

        total = None
        for group in parts:
            f = jnp.concatenate([factor(half, k) for half, k in group], axis=0)
            x = tuple(
                jnp.concatenate([ref[k, half] for half, k in group], axis=0) for ref in (xhi, xlo)
            )
            term = dot3(split(f), x, ((0,), (0,)))
            total = term if total is None else total + term
        rows = pl.ds(pl.multiple_of(block * NB, NB), NB)
        out[rows, :] = out[rows, :] - total

    def all_blocks(parts):
        def blocks(block, carry):
            update(block, parts)
            return carry

        lax.fori_loop(1 - row // OWNERS, 4, blocks, 0)

    own_half = big.at[1 - q, xh]
    pltpu.make_async_copy(own_half, own_half, sib_r.at[1]).wait()
    all_blocks((((xh, 0), (xh, 1)), ((xh, 2), (xh, 3))))
    rest = big.at[1 - q, 1 - xh, :, REST]
    pltpu.make_async_copy(rest, rest, sib_r.at[3]).wait()
    all_blocks((((1 - xh, 0), (1 - xh, 1)), ((1 - xh, 2), (1 - xh, 3))))

    def left(kind, ref):
        pltpu.make_async_copy(ref, ref, send.at[kind]).wait()

    most = pl.ds(0, NZ - 1)
    left(RING, big.at[q, xh, most])
    left(TREE, small.at[q, y, most])
    left(Y, small.at[q, pl.ds(0, 2)])
    left(RELAY, small.at[q, 0])
    left(X, big.at[q, xh, :, REST])
    left(SIB, big.at[q, xh])
    left(SIB_SMALL, small.at[q])
    left(SIB_PEER, big.at[q, 1 - xh, :, REST])

    for k in (1, 2, 3):

        @pl.when(row == k)
        def _(k=k):
            src, dst = chain(k, xh)
            for i, device in enumerate(alike):
                remote(src, dst, ch_s.at[i], ch_r.at[xh], device).wait_send()

    for quarter in (0, 1):

        @pl.when(y == quarter)
        def _(quarter=quarter):
            src, dst = inverse_part(quarter, xh)
            remote(src, dst, ch_s.at[3], ch_r.at[2], peer).wait_send()

    for part in (0, 1):
        ref = b_half(bvec.at[0], part)
        for i in range(3):
            remote(ref, ref, b_s.at[i, part], b_r.at[0, part], peer).wait_send()

    @pl.when(row < OWNERS)
    def _():
        for part in (0, 1):
            b_cross(0, part).wait_send()


def per_device(right_side, factor_panels, inverses):
    rows, columns = right_side.shape
    dma = pltpu.SemaphoreType.DMA
    return pl.pallas_call(
        kernel,
        name="solve",
        out_shape=pltpu.VMEM((rows, columns), F32),
        in_specs=[pl.BlockSpec(memory_space=pltpu.HBM)] * 3,
        out_specs=pl.BlockSpec(memory_space=pltpu.VMEM),
        scratch_shapes=[
            pltpu.VMEM((2, 2, NZ, PANELS, 4, rows), F32),
            pltpu.VMEM((2, 4, NZ, 2, SLOTS, 4, NB), F32),
            pltpu.VMEM((OWNERS, NB, columns), F32),
            pltpu.VMEM((PANELS, 2, HALF, columns), BF16),
            pltpu.VMEM((PANELS, 2, HALF, columns), BF16),
            pltpu.VMEM((4 * SLOTS, NB, NB), BF16),
            pltpu.VMEM((4 * SLOTS, NB, NB), BF16),
            dma((8,)),
            dma((2, 8, len(CHUNKS))),
            dma((2, 8, 2)),
            dma((3, 2, 9, 2)),
            dma((2, 9)),
            dma((4,)),
            dma((4,)),
            dma((4,)),
            dma((4, 2)),
            dma((4, 2)),
            dma((2,)),
        ],
        compiler_params=pltpu.CompilerParams(
            collective_id=0, has_side_effects=True, vmem_limit_bytes=62 << 20
        ),
        cost_estimate=pl.CostEstimate(flops=1 << 31, bytes_accessed=8 << 20, transcendentals=0),
    )(right_side, factor_panels, inverses)


def solution(mesh):
    in_specs = (P("row", "col"), P(None, "col", "row"), P(None, "col", None))
    return jax.shard_map(
        per_device, mesh=mesh, in_specs=in_specs, out_specs=P("row", "col"), check_vma=False
    )
```

```python
import jax
import jax.numpy as jnp
from jax import lax
from jax.experimental import pallas as pl
from jax.experimental.pallas import tpu as pltpu
from jax.sharding import PartitionSpec as P

MESH = pl.DeviceIdType.MESH
NZ = 16
PANELS = 4
OWNERS = 4
NB = 256
HALF = 128
CHUNKS = ((0, 2), (2, 2))
SLOTS = 3
BF16 = jnp.bfloat16
F32 = jnp.float32

def block_place(m, k):
    return SLOTS * k + m


def inverse_place(k):
    return k + k // 3


RING, TREE, Y, RELAY, X, SIB, SIB_SMALL, SIB_PEER = range(8)


def split(value):
    high = value.astype(BF16)
    low = (value - high.astype(F32)).astype(BF16)
    return high, low


def dot3(a, b, dims):
    def one(p, q):
        return lax.dot_general(p, q, (dims, ((), ())), preferred_element_type=F32)

    return one(a[0], b[0]) + (one(a[0], b[1]) + one(a[1], b[0]))


def kernel(
    rs_hbm, fac, inv, out,
    big, small, bvec, xhi, xlo, ahi, alo,
    send, ring_r, tree_r, y_r, x_r, sib_r,
    ch_s, ch_r, b_s, b_r, loc_s,
):
    row = lax.axis_index("row")
    col = lax.axis_index("col")
    y = row % 4
    xh, z, q = col // 32, (col // 2) % NZ, col % 2

    def at(row_to, xh_to, z_to, q_to):
        return (row_to, (xh_to * NZ + z_to) * 2 + q_to)

    def along_z(hop):
        return at(row, xh, (z + NZ + hop) % NZ, q)

    def along_y(hop):
        return at((row // 4) * 4 + (y + 4 + hop) % 4, xh, z, q)

    sibling = at(row, xh, z, 1 - q)
    peer = at(row, 1 - xh, z, q)
    alike = [at((row + 4 * (i % 2)) % 8, (xh + i // 2) % 2, z, q) for i in (1, 2, 3)]
    across_y = [along_y(1), along_y(-1)]
    before, after, over = (y + 3) % 4, (y + 1) % 4, (y + 2) % 4

    own_big = pltpu.make_async_copy(fac, big.at[q, xh, z], loc_s.at[1])
    own_big.start()
    load_rs = pltpu.make_async_copy(rs_hbm, out, loc_s.at[0])
    load_rs.start()

    barrier = pltpu.get_barrier_semaphore()
    greet = [along_z(hop) for hop in (1, -1, 2, -2)] + [sibling] + alike + across_y
    for device in greet:
        pl.semaphore_signal(barrier, inc=1, device_id=device, device_id_type=MESH)
    pl.semaphore_wait(barrier, len(greet))

    def remote(src, dst, send, recv, device):
        return pltpu.make_async_remote_copy(
            src_ref=src, dst_ref=dst, send_sem=send, recv_sem=recv,
            device_id=device, device_id_type=MESH,
        )

    def origin_of(distance, d):
        return (z + NZ - distance) % NZ if d == 0 else (z + distance) % NZ

    def chunk(origin, c):
        return big.at[q, xh, origin, pl.ds(CHUNKS[c][0], CHUNKS[c][1])]

    def hop_to(hop, d):
        return along_z(hop if d == 0 else -hop)

    def grow(held, hop, d, c):
        ref = chunk(origin_of(held, d), c)
        return remote(ref, ref, send.at[RING], ring_r.at[d, held + hop - 1, c], hop_to(hop, d))

    def arrival(distance, d, c):
        ref = chunk(origin_of(distance, d), c)
        return remote(ref, ref, send.at[RING], ring_r.at[d, distance - 1, c], hop_to(1, d))

    def to_sibling(origin, slot, d, c):
        ref = chunk(origin, c)
        return remote(ref, ref, send.at[SIB], sib_r.at[1], sibling)

    def to_peer(origin, slot, d, c):
        ref = chunk(origin, c)
        return remote(ref, ref, send.at[X], x_r.at[d, slot], peer)

    def peer_part(origin, part):
        return big.at[q, 1 - xh, origin, part]

    def from_peer(origin, slot, d, part):
        ref = peer_part(origin, part)
        return remote(ref, ref, send.at[SIB_PEER], x_r.at[d, slot], peer)

    def peer_to_sibling(origin, slot, d, part):
        ref = peer_part(origin, part)
        return remote(ref, ref, send.at[SIB_PEER], sib_r.at[3], sibling)

    REST, ONE, TWO = pl.ds(0, 4), pl.ds(0, 2), pl.ds(2, 2)

    def last_leaves(d, c):
        return (d == 1) == (CHUNKS[c][0] >= 2)

    LAST = [(d, c) for c in range(len(CHUNKS)) for d in (0, 1) if last_leaves(d, c)]

    def hand_on(distance, d, c):
        origin = origin_of(distance, d)
        to_peer(origin, distance, d, c).start()
        to_sibling(origin, distance, d, c).start()

    def take_end(distance, d, c):
        arrival(distance, d, c).wait_recv()
        hand_on(distance, d, c)

    def peer_arrivals(step):
        for d in (0, 1):
            origin = origin_of(step, d)
            from_peer(origin, step, d, REST).wait_recv()
            peer_to_sibling(origin, step, d, REST).start()

    def small_part(quarter, origin, h):
        return small.at[q, quarter, origin, h]

    def tree(held, hop, d, h):
        ref = small_part(y, origin_of(held, d), h)
        to = held + hop - 1
        return remote(ref, ref, send.at[TREE], tree_r.at[d, to, h], along_z(hop if d == 0 else -hop))

    def small_arrival(distance, d, h):
        ref = small_part(y, origin_of(distance, d), h)
        return remote(ref, ref, send.at[TREE], tree_r.at[d, distance - 1, h], along_z(1))

    def small_to_y(distance, d, h, i):
        ref = small_part(y, origin_of(distance, d), h)
        return remote(ref, ref, send.at[Y], y_r.at[i, d, distance, h], across_y[i])

    def small_to_sibling(distance, d, h):
        ref = small_part(y, origin_of(distance, d), h)
        return remote(ref, ref, send.at[SIB_SMALL], sib_r.at[0], sibling)

    def y_arrival(distance, d, h, i):
        ref = small_part((before, after, over)[i], origin_of(distance, d), h)
        return remote(ref, ref, send.at[SIB_SMALL], y_r.at[i, d, distance, h], sibling)

    def y_to_sibling(distance, d, h, i):
        ref = small_part((before, after, over)[i], origin_of(distance, d), h)
        return remote(ref, ref, send.at[SIB_SMALL], sib_r.at[0], sibling)

    def relay(distance, d, h):
        ref = small_part((before, after)[h], origin_of(distance, d), h)
        return remote(ref, ref, send.at[RELAY], y_r.at[2, d, distance, h], across_y[h])

    def spread(distance, d, h):
        for i in (0, 1):
            small_to_y(distance, d, h, i).start()
        small_to_sibling(distance, d, h).start()

    def take_odd(distance, d, h):
        small_arrival(distance, d, h).wait_recv()
        spread(distance, d, h)

    def take_y(distance, d, h):
        for i in (0, 1):
            y_arrival(distance, d, h, i).wait_recv()
            if i == h:
                relay(distance, d, h).start()
            y_to_sibling(distance, d, h, i).start()

    def take_over(distance, d, h):
        y_arrival(distance, d, h, 2).wait_recv()
        y_to_sibling(distance, d, h, 2).start()

    def chain(k, h):
        return fac.at[pl.ds(0, k), :, pl.ds(0, NB)], small.at[q, k, z, h, pl.ds(0, k)]

    for k in (1, 2, 3):

        @pl.when(row == k)
        def _(k=k):
            src, dst = chain(k, xh)
            for i, device in enumerate(alike):
                remote(src, dst, ch_s.at[i], ch_r.at[xh], device).start()
            pltpu.make_async_copy(src, dst, ch_r.at[xh]).start()

    def inverse_part(quarter, h):
        src = inv.at[pl.ds(0, 3)] if quarter == 0 else inv.at[pl.ds(3, 1)]
        return src, small.at[q, quarter, z, h, pl.ds(0, 3) if quarter == 0 else pl.ds(1, 1)]

    for quarter in (0, 1):

        @pl.when(y == quarter)
        def _(quarter=quarter):
            src, dst = inverse_part(quarter, xh)
            remote(src, dst, ch_s.at[3], ch_r.at[2], peer).start()
            pltpu.make_async_copy(src, dst, ch_r.at[3]).start()

    @pl.when((y == 1) | (y == 2))
    def _():
        for h in (0, 1):
            small[q, y, z, h, 2] = jnp.zeros((4, NB), F32)

    def b_half(ref, part):
        return ref.at[pl.ds(part * HALF, HALF)]

    def b_cross(k, part):
        return remote(
            b_half(rs_hbm, part), b_half(bvec.at[k], part), b_s.at[3, part], b_r.at[k, part], at(k + 4, xh, z, q)
        )

    for k in range(OWNERS):

        @pl.when(row == k)
        def _(k=k):
            for part in (0, 1):
                b_cross(k, part).start()

    own_big.wait()
    for c in range(len(CHUNKS)):
        for d in (0, 1):
            grow(0, 2, d, c).start()
            grow(0, 1, d, c).start()
    for c in range(len(CHUNKS)):
        to_peer(z, 0, 0, c).start()
        to_sibling(z, 0, 0, c).start()

    for k in range(OWNERS):

        @pl.when(row == k)
        def _(k=k):
            for part in (0, 1):
                for i in (0, 1):
                    remote(
                        b_half(rs_hbm, part), b_half(bvec.at[k], part), b_s.at[i, part], b_r.at[k, part], across_y[i]
                    ).start()
                pltpu.make_async_copy(
                    b_half(rs_hbm, part), b_half(bvec.at[k], part), b_r.at[k, part]
                ).start()

    def b_wait(k, part):
        pltpu.make_async_copy(b_half(rs_hbm, part), b_half(bvec.at[k], part), b_r.at[k, part]).wait()

    def forward_b(part):
        for k in range(OWNERS):

            @pl.when(row == OWNERS + k)
            def _(k=k):
                b_wait(k, part)
                ref = b_half(bvec.at[k], part)
                for i in (0, 1):
                    remote(ref, ref, b_s.at[i, part], b_r.at[k, part], across_y[i]).start()

    def relay_b(part):
        k = (before, after)[part]
        b_wait(k, part)
        ref = b_half(bvec.at[k], part)
        remote(ref, ref, b_s.at[2, part], b_r.at[k, part], across_y[part]).start()

    for quarter in (0, 1):

        @pl.when(y == quarter)
        def _(quarter=quarter):
            for sem, h in ((ch_r.at[3], xh), (ch_r.at[2], 1 - xh)):
                src, dst = inverse_part(quarter, h)
                pltpu.make_async_copy(src, dst, sem).wait()

    for k in (1, 2, 3):

        @pl.when(y == k)
        def _(k=k):
            for h in (0, 1):
                src, dst = chain(k, h)
                pltpu.make_async_copy(src, dst, ch_r.at[h]).wait()

    for h in (0, 1):
        for d in (0, 1):
            tree(0, 2, d, h).start()
            tree(0, 1, d, h).start()
        spread(0, 0, h)

    def steps(j, carry):
        for h in (0, 1):
            for d in (0, 1):
                small_arrival(2 * j, d, h).wait_recv()
                if h == d:
                    tree(2 * j, 2, d, h).start()
                else:

                    @pl.when(j < 3)
                    def _(d=d, h=h):
                        tree(2 * j, 2, d, h).start()

                tree(2 * j, 1, d, h).start()
                spread(2 * j, d, h)
        for c in range(len(CHUNKS)):
            for d in (0, 1):
                arrival(2 * j, d, c).wait_recv()
                if last_leaves(d, c):
                    grow(2 * j, 2, d, c).start()
                else:

                    @pl.when(j < 3)
                    def _(d=d, c=c):
                        grow(2 * j, 2, d, c).start()

                grow(2 * j, 1, d, c).start()
                hand_on(2 * j, d, c)
        for h in (0, 1):
            for d in (0, 1):
                take_odd(2 * j - 1, d, h)

        @pl.when(j == 1)
        def _():
            from_peer(z, 0, 0, REST).wait_recv()
            peer_to_sibling(z, 0, 0, REST).start()
            forward_b(0)
            for h in (0, 1):
                take_y(0, 0, h)

        @pl.when(j > 1)
        def _():
            for h in (0, 1):
                for d in (0, 1):
                    take_y(2 * j - 3, d, h)
                    take_y(2 * j - 2, d, h)

        @pl.when(j == 2)
        def _():
            forward_b(1)
            for h in (0, 1):
                take_over(0, 0, h)

        @pl.when(j == 3)
        def _():
            for part in (0, 1):
                relay_b(part)
            for h in (0, 1):
                for d in (0, 1):
                    take_over(1, d, h)
                    take_over(2, d, h)

        for c in range(len(CHUNKS)):
            for d in (0, 1):
                take_end(2 * j - 1, d, c)

        @pl.when(j > 1)
        def _():
            peer_arrivals(2 * j - 3)
            peer_arrivals(2 * j - 2)

        return carry

    lax.fori_loop(1, 4, steps, 0)
    for h in (0, 1):
        take_odd(8, h, h)
    for h in (0, 1):
        for d in (0, 1):
            take_odd(7, d, h)
    for h in (0, 1):
        for d in (0, 1):
            take_y(5, d, h)
            take_y(6, d, h)
    for d, c in LAST:
        take_end(8, d, c)
    for h in (0, 1):
        for d in (0, 1):
            take_over(3, d, h)
            take_over(4, d, h)
    for h in (0, 1):
        take_y(8, h, h)
        for d in (0, 1):
            take_y(7, d, h)
    for c in range(len(CHUNKS)):
        for d in (0, 1):
            take_end(7, d, c)
    for h in (0, 1):
        for d in (0, 1):
            take_over(5, d, h)
            take_over(6, d, h)
    for h in (0, 1):
        take_over(8, h, h)
        for d in (0, 1):
            take_over(7, d, h)

    @pl.when(row < OWNERS)
    def _():
        for part in (0, 1):
            b_wait(y, part)

    b_wait(before, 1)
    b_wait(after, 0)
    for part in (0, 1):
        b_wait(over, part)

    work = [bvec[k].T for k in range(PANELS)]

    sib_small = small.at[1 - q]
    pltpu.make_async_copy(sib_small, sib_small, sib_r.at[0]).wait()

    def prepare(place, carry):
        quarter, slot = place // SLOTS, place % SLOTS
        for half in (0, 1):
            value = jnp.concatenate(
                [small[0, quarter, :, half, slot], small[1, quarter, :, half, slot]], axis=1
            ).reshape(HALF, NB)
            ahi[place, pl.ds(half * HALF, HALF), :], alo[place, pl.ds(half * HALF, HALF), :] = split(value)
        return carry

    lax.fori_loop(0, 5, prepare, 0)
    lax.fori_loop(6, 8, prepare, 0)
    lax.fori_loop(9, 12, prepare, 0)
    load_rs.wait()

    for k in range(PANELS):
        place = inverse_place(k)
        answer = dot3(split(work[k]), (ahi[place], alo[place]), ((1,), (1,)))
        x = split(answer)
        for m in range(k + 1, PANELS):
            place = block_place(k, m)
            work[m] = work[m] - dot3(x, (ahi[place], alo[place]), ((1,), (0,)))

        @pl.when(row == k)
        def _(answer=answer):
            out[pl.ds(0, NB), :] = answer.T

        for half in (0, 1):
            xhi[k, half] = x[0][:, half * HALF : (half + 1) * HALF]
            xlo[k, half] = x[1][:, half * HALF : (half + 1) * HALF]
        if k == 1:
            peer_arrivals(5)
            peer_arrivals(6)
            peer_arrivals(7)
    for d, part in ((0, ONE), (1, TWO)):
        origin = origin_of(8, d)
        from_peer(origin, 8, d, part).wait_recv()
        peer_to_sibling(origin, 8, d, part).start()

    def update(block, parts):
        lanes = pl.ds(pl.multiple_of(block * NB, NB), NB)

        def factor(half, k):
            return jnp.concatenate(
                [big[0, half, :, k, :, lanes], big[1, half, :, k, :, lanes]], axis=1
            ).reshape(HALF, NB)

        total = None
        for group in parts:
            f = jnp.concatenate([factor(half, k) for half, k in group], axis=0)
            x = tuple(
                jnp.concatenate([ref[k, half] for half, k in group], axis=1) for ref in (xhi, xlo)
            )
            term = dot3(x, split(f), ((1,), (0,)))
            total = term if total is None else total + term
        rows = pl.ds(pl.multiple_of(block * NB, NB), NB)
        out[rows, :] = out[rows, :] - total.T

    def all_blocks(parts):
        def blocks(block, carry):
            update(block, parts)
            return carry

        lax.fori_loop(1 - row // OWNERS, 4, blocks, 0)

    own_half = big.at[1 - q, xh]
    pltpu.make_async_copy(own_half, own_half, sib_r.at[1]).wait()
    all_blocks((((xh, 0), (xh, 1)), ((xh, 2), (xh, 3))))
    rest = big.at[1 - q, 1 - xh, :, REST]
    pltpu.make_async_copy(rest, rest, sib_r.at[3]).wait()
    all_blocks((((1 - xh, 0), (1 - xh, 1)), ((1 - xh, 2), (1 - xh, 3))))

    def left(kind, ref):
        pltpu.make_async_copy(ref, ref, send.at[kind]).wait()

    most = pl.ds(0, NZ - 1)
    left(RING, big.at[q, xh, most])
    left(TREE, small.at[q, y, most])
    left(Y, small.at[q, pl.ds(0, 2)])
    left(RELAY, small.at[q, 0])
    left(X, big.at[q, xh, :, REST])
    left(SIB, big.at[q, xh])
    left(SIB_SMALL, small.at[q])
    left(SIB_PEER, big.at[q, 1 - xh, :, REST])

    for k in (1, 2, 3):

        @pl.when(row == k)
        def _(k=k):
            src, dst = chain(k, xh)
            for i, device in enumerate(alike):
                remote(src, dst, ch_s.at[i], ch_r.at[xh], device).wait_send()

    for quarter in (0, 1):

        @pl.when(y == quarter)
        def _(quarter=quarter):
            src, dst = inverse_part(quarter, xh)
            remote(src, dst, ch_s.at[3], ch_r.at[2], peer).wait_send()

    for part in (0, 1):
        ref = b_half(bvec.at[0], part)
        for i in range(3):
            remote(ref, ref, b_s.at[i, part], b_r.at[0, part], peer).wait_send()

    @pl.when(row < OWNERS)
    def _():
        for part in (0, 1):
            b_cross(0, part).wait_send()


def per_device(right_side, factor_panels, inverses):
    rows, columns = right_side.shape
    dma = pltpu.SemaphoreType.DMA
    return pl.pallas_call(
        kernel,
        name="solve",
        out_shape=pltpu.VMEM((rows, columns), F32),
        in_specs=[pl.BlockSpec(memory_space=pltpu.HBM)] * 3,
        out_specs=pl.BlockSpec(memory_space=pltpu.VMEM),
        scratch_shapes=[
            pltpu.VMEM((2, 2, NZ, PANELS, 4, rows), F32),
            pltpu.VMEM((2, 4, NZ, 2, SLOTS, 4, NB), F32),
            pltpu.VMEM((OWNERS, NB, columns), F32),
            pltpu.VMEM((PANELS, 2, columns, HALF), BF16),
            pltpu.VMEM((PANELS, 2, columns, HALF), BF16),
            pltpu.VMEM((4 * SLOTS, NB, NB), BF16),
            pltpu.VMEM((4 * SLOTS, NB, NB), BF16),
            dma((8,)),
            dma((2, 8, len(CHUNKS))),
            dma((2, 8, 2)),
            dma((3, 2, 9, 2)),
            dma((2, 9)),
            dma((4,)),
            dma((4,)),
            dma((4,)),
            dma((4, 2)),
            dma((4, 2)),
            dma((2,)),
        ],
        compiler_params=pltpu.CompilerParams(
            collective_id=0, has_side_effects=True, vmem_limit_bytes=62 << 20
        ),
        cost_estimate=pl.CostEstimate(flops=1 << 31, bytes_accessed=8 << 20, transcendentals=0),
    )(right_side, factor_panels, inverses)


def solution(mesh):
    in_specs = (P("row", "col"), P(None, "col", "row"), P(None, "col", None))
    return jax.shard_map(
        per_device, mesh=mesh, in_specs=in_specs, out_specs=P("row", "col"), check_vma=False
    )
```

```python
import jax
import jax.numpy as jnp
from jax import lax
from jax.experimental import pallas as pl
from jax.experimental.pallas import tpu as pltpu
from jax.sharding import PartitionSpec as P

MESH = pl.DeviceIdType.MESH
NZ = 16
PANELS = 4
OWNERS = 4
NB = 256
HALF = 128
CHUNKS = ((0, 2), (2, 2))
SLOTS = 3
BF16 = jnp.bfloat16
F32 = jnp.float32

def block_place(m, k):
    return SLOTS * k + m


def inverse_place(k):
    return k + k // 3


RING, TREE, Y, RELAY, X, SIB, SIB_SMALL, SIB_PEER = range(8)


def split(value):
    high = value.astype(BF16)
    low = (value - high.astype(F32)).astype(BF16)
    return high, low


def dot3(a, b, dims):
    def one(p, q):
        return lax.dot_general(p, q, (dims, ((), ())), preferred_element_type=F32)

    return one(a[0], b[0]) + (one(a[0], b[1]) + one(a[1], b[0]))


def kernel(
    rs_hbm, fac, inv, out,
    big, small, bvec, xhi, xlo, ahi, alo,
    send, ring_r, tree_r, y_r, x_r, sib_r,
    ch_s, ch_r, b_s, b_r, loc_s,
):
    row = lax.axis_index("row")
    col = lax.axis_index("col")
    y = row % 4
    xh, z, q = col // 32, (col // 2) % NZ, col % 2

    def at(row_to, xh_to, z_to, q_to):
        return (row_to, (xh_to * NZ + z_to) * 2 + q_to)

    def along_z(hop):
        return at(row, xh, (z + NZ + hop) % NZ, q)

    def along_y(hop):
        return at((row // 4) * 4 + (y + 4 + hop) % 4, xh, z, q)

    sibling = at(row, xh, z, 1 - q)
    peer = at(row, 1 - xh, z, q)
    alike = [at((row + 4 * (i % 2)) % 8, (xh + i // 2) % 2, z, q) for i in (1, 2, 3)]
    across_y = [along_y(1), along_y(-1)]
    before, after, over = (y + 3) % 4, (y + 1) % 4, (y + 2) % 4

    own_big = pltpu.make_async_copy(fac, big.at[q, xh, z], loc_s.at[1])
    own_big.start()
    load_rs = pltpu.make_async_copy(rs_hbm, out, loc_s.at[0])
    load_rs.start()

    barrier = pltpu.get_barrier_semaphore()
    greet = [along_z(hop) for hop in (1, -1, 2, -2)] + [sibling] + alike + across_y
    for device in greet:
        pl.semaphore_signal(barrier, inc=1, device_id=device, device_id_type=MESH)
    pl.semaphore_wait(barrier, len(greet))

    def remote(src, dst, send, recv, device):
        return pltpu.make_async_remote_copy(
            src_ref=src, dst_ref=dst, send_sem=send, recv_sem=recv,
            device_id=device, device_id_type=MESH,
        )

    def origin_of(distance, d):
        return (z + NZ - distance) % NZ if d == 0 else (z + distance) % NZ

    def chunk(origin, c):
        return big.at[q, xh, origin, pl.ds(CHUNKS[c][0], CHUNKS[c][1])]

    def hop_to(hop, d):
        return along_z(hop if d == 0 else -hop)

    def grow(held, hop, d, c):
        ref = chunk(origin_of(held, d), c)
        return remote(ref, ref, send.at[RING], ring_r.at[d, held + hop - 1, c], hop_to(hop, d))

    def arrival(distance, d, c):
        ref = chunk(origin_of(distance, d), c)
        return remote(ref, ref, send.at[RING], ring_r.at[d, distance - 1, c], hop_to(1, d))

    def to_sibling(origin, slot, d, c):
        ref = chunk(origin, c)
        return remote(ref, ref, send.at[SIB], sib_r.at[1], sibling)

    def to_peer(origin, slot, d, c):
        ref = chunk(origin, c)
        return remote(ref, ref, send.at[X], x_r.at[d, slot], peer)

    def peer_part(origin, part):
        return big.at[q, 1 - xh, origin, part]

    def from_peer(origin, slot, d, part):
        ref = peer_part(origin, part)
        return remote(ref, ref, send.at[SIB_PEER], x_r.at[d, slot], peer)

    def peer_to_sibling(origin, slot, d, part):
        ref = peer_part(origin, part)
        return remote(ref, ref, send.at[SIB_PEER], sib_r.at[3], sibling)

    REST, ONE, TWO = pl.ds(0, 4), pl.ds(0, 2), pl.ds(2, 2)

    def last_leaves(d, c):
        return (d == 1) == (CHUNKS[c][0] >= 2)

    LAST = [(d, c) for c in range(len(CHUNKS)) for d in (0, 1) if last_leaves(d, c)]

    def hand_on(distance, d, c):
        origin = origin_of(distance, d)
        to_peer(origin, distance, d, c).start()
        to_sibling(origin, distance, d, c).start()

    def take_end(distance, d, c):
        arrival(distance, d, c).wait_recv()
        hand_on(distance, d, c)

    def peer_arrivals(step):
        for d in (0, 1):
            origin = origin_of(step, d)
            from_peer(origin, step, d, REST).wait_recv()
            peer_to_sibling(origin, step, d, REST).start()

    def small_part(quarter, origin, h):
        return small.at[q, quarter, origin, h]

    def tree(held, hop, d, h):
        ref = small_part(y, origin_of(held, d), h)
        to = held + hop - 1
        return remote(ref, ref, send.at[TREE], tree_r.at[d, to, h], along_z(hop if d == 0 else -hop))

    def small_arrival(distance, d, h):
        ref = small_part(y, origin_of(distance, d), h)
        return remote(ref, ref, send.at[TREE], tree_r.at[d, distance - 1, h], along_z(1))

    def small_to_y(distance, d, h, i):
        ref = small_part(y, origin_of(distance, d), h)
        return remote(ref, ref, send.at[Y], y_r.at[i, d, distance, h], across_y[i])

    def small_to_sibling(distance, d, h):
        ref = small_part(y, origin_of(distance, d), h)
        return remote(ref, ref, send.at[SIB_SMALL], sib_r.at[0], sibling)

    def y_arrival(distance, d, h, i):
        ref = small_part((before, after, over)[i], origin_of(distance, d), h)
        return remote(ref, ref, send.at[SIB_SMALL], y_r.at[i, d, distance, h], sibling)

    def y_to_sibling(distance, d, h, i):
        ref = small_part((before, after, over)[i], origin_of(distance, d), h)
        return remote(ref, ref, send.at[SIB_SMALL], sib_r.at[0], sibling)

    def relay(distance, d, h):
        ref = small_part((before, after)[h], origin_of(distance, d), h)
        return remote(ref, ref, send.at[RELAY], y_r.at[2, d, distance, h], across_y[h])

    def spread(distance, d, h):
        for i in (0, 1):
            small_to_y(distance, d, h, i).start()
        small_to_sibling(distance, d, h).start()

    def take_odd(distance, d, h):
        small_arrival(distance, d, h).wait_recv()
        spread(distance, d, h)

    def take_y(distance, d, h):
        for i in (0, 1):
            y_arrival(distance, d, h, i).wait_recv()
            if i == h:
                relay(distance, d, h).start()
            y_to_sibling(distance, d, h, i).start()

    def take_over(distance, d, h):
        y_arrival(distance, d, h, 2).wait_recv()
        y_to_sibling(distance, d, h, 2).start()

    def chain(k, h):
        return fac.at[pl.ds(0, k), :, pl.ds(0, NB)], small.at[q, k, z, h, pl.ds(0, k)]

    for k in (1, 2, 3):

        @pl.when(row == k)
        def _(k=k):
            src, dst = chain(k, xh)
            for i, device in enumerate(alike):
                remote(src, dst, ch_s.at[i], ch_r.at[xh], device).start()
            pltpu.make_async_copy(src, dst, ch_r.at[xh]).start()

    def inverse_part(quarter, h):
        src = inv.at[pl.ds(0, 3)] if quarter == 0 else inv.at[pl.ds(3, 1)]
        return src, small.at[q, quarter, z, h, pl.ds(0, 3) if quarter == 0 else pl.ds(1, 1)]

    for quarter in (0, 1):

        @pl.when(y == quarter)
        def _(quarter=quarter):
            src, dst = inverse_part(quarter, xh)
            remote(src, dst, ch_s.at[3], ch_r.at[2], peer).start()
            pltpu.make_async_copy(src, dst, ch_r.at[3]).start()

    @pl.when((y == 1) | (y == 2))
    def _():
        for h in (0, 1):
            small[q, y, z, h, 2] = jnp.zeros((4, NB), F32)

    def b_half(ref, part):
        return ref.at[pl.ds(part * HALF, HALF)]

    def b_cross(k, part):
        return remote(
            b_half(rs_hbm, part), b_half(bvec.at[k], part), b_s.at[3, part], b_r.at[k, part], at(k + 4, xh, z, q)
        )

    for k in range(OWNERS):

        @pl.when(row == k)
        def _(k=k):
            for part in (0, 1):
                b_cross(k, part).start()

    own_big.wait()
    for c in range(len(CHUNKS)):
        for d in (0, 1):
            grow(0, 2, d, c).start()
            grow(0, 1, d, c).start()
    for c in range(len(CHUNKS)):
        to_peer(z, 0, 0, c).start()
        to_sibling(z, 0, 0, c).start()

    for k in range(OWNERS):

        @pl.when(row == k)
        def _(k=k):
            for part in (0, 1):
                for i in (0, 1):
                    remote(
                        b_half(rs_hbm, part), b_half(bvec.at[k], part), b_s.at[i, part], b_r.at[k, part], across_y[i]
                    ).start()
                pltpu.make_async_copy(
                    b_half(rs_hbm, part), b_half(bvec.at[k], part), b_r.at[k, part]
                ).start()

    def b_wait(k, part):
        pltpu.make_async_copy(b_half(rs_hbm, part), b_half(bvec.at[k], part), b_r.at[k, part]).wait()

    def forward_b(part):
        for k in range(OWNERS):

            @pl.when(row == OWNERS + k)
            def _(k=k):
                b_wait(k, part)
                ref = b_half(bvec.at[k], part)
                for i in (0, 1):
                    remote(ref, ref, b_s.at[i, part], b_r.at[k, part], across_y[i]).start()

    def relay_b(part):
        k = (before, after)[part]
        b_wait(k, part)
        ref = b_half(bvec.at[k], part)
        remote(ref, ref, b_s.at[2, part], b_r.at[k, part], across_y[part]).start()

    for quarter in (0, 1):

        @pl.when(y == quarter)
        def _(quarter=quarter):
            for sem, h in ((ch_r.at[3], xh), (ch_r.at[2], 1 - xh)):
                src, dst = inverse_part(quarter, h)
                pltpu.make_async_copy(src, dst, sem).wait()

    for k in (1, 2, 3):

        @pl.when(y == k)
        def _(k=k):
            for h in (0, 1):
                src, dst = chain(k, h)
                pltpu.make_async_copy(src, dst, ch_r.at[h]).wait()

    for h in (0, 1):
        for d in (0, 1):
            tree(0, 2, d, h).start()
            tree(0, 1, d, h).start()
        spread(0, 0, h)

    def steps(j, carry):
        for h in (0, 1):
            for d in (0, 1):
                small_arrival(2 * j, d, h).wait_recv()
                if h == d:
                    tree(2 * j, 2, d, h).start()
                else:

                    @pl.when(j < 3)
                    def _(d=d, h=h):
                        tree(2 * j, 2, d, h).start()

                tree(2 * j, 1, d, h).start()
                spread(2 * j, d, h)
        for c in range(len(CHUNKS)):
            for d in (0, 1):
                arrival(2 * j, d, c).wait_recv()
                if last_leaves(d, c):
                    grow(2 * j, 2, d, c).start()
                else:

                    @pl.when(j < 3)
                    def _(d=d, c=c):
                        grow(2 * j, 2, d, c).start()

                grow(2 * j, 1, d, c).start()
                hand_on(2 * j, d, c)
        for h in (0, 1):
            for d in (0, 1):
                take_odd(2 * j - 1, d, h)

        @pl.when(j == 1)
        def _():
            from_peer(z, 0, 0, REST).wait_recv()
            peer_to_sibling(z, 0, 0, REST).start()
            forward_b(0)
            forward_b(1)
            for h in (0, 1):
                take_y(0, 0, h)

        @pl.when(j > 1)
        def _():
            for h in (0, 1):
                for d in (0, 1):
                    take_y(2 * j - 3, d, h)
                    take_y(2 * j - 2, d, h)

        @pl.when(j == 2)
        def _():
            for part in (0, 1):
                relay_b(part)
            for h in (0, 1):
                take_over(0, 0, h)

        @pl.when(j == 3)
        def _():
            for h in (0, 1):
                for d in (0, 1):
                    take_over(1, d, h)
                    take_over(2, d, h)

        for c in range(len(CHUNKS)):
            for d in (0, 1):
                take_end(2 * j - 1, d, c)

        @pl.when(j > 1)
        def _():
            peer_arrivals(2 * j - 3)
            peer_arrivals(2 * j - 2)

        return carry

    lax.fori_loop(1, 4, steps, 0)
    for h in (0, 1):
        take_odd(8, h, h)
    for h in (0, 1):
        for d in (0, 1):
            take_odd(7, d, h)
    for h in (0, 1):
        for d in (0, 1):
            take_y(5, d, h)
            take_y(6, d, h)
    for d, c in LAST:
        take_end(8, d, c)
    for h in (0, 1):
        for d in (0, 1):
            take_over(3, d, h)
            take_over(4, d, h)
    for h in (0, 1):
        take_y(8, h, h)
        for d in (0, 1):
            take_y(7, d, h)
    for c in range(len(CHUNKS)):
        for d in (0, 1):
            take_end(7, d, c)
    for h in (0, 1):
        for d in (0, 1):
            take_over(5, d, h)
            take_over(6, d, h)
    for h in (0, 1):
        take_over(8, h, h)
        for d in (0, 1):
            take_over(7, d, h)

    @pl.when(row < OWNERS)
    def _():
        for part in (0, 1):
            b_wait(y, part)

    b_wait(before, 1)
    b_wait(after, 0)
    for part in (0, 1):
        b_wait(over, part)

    work = [bvec[k].T for k in range(PANELS)]

    sib_small = small.at[1 - q]
    pltpu.make_async_copy(sib_small, sib_small, sib_r.at[0]).wait()

    def prepare(place, carry):
        quarter, slot = place // SLOTS, place % SLOTS
        for half in (0, 1):
            value = jnp.concatenate(
                [small[0, quarter, :, half, slot], small[1, quarter, :, half, slot]], axis=1
            ).reshape(HALF, NB)
            ahi[place, pl.ds(half * HALF, HALF), :], alo[place, pl.ds(half * HALF, HALF), :] = split(value)
        return carry

    lax.fori_loop(0, 5, prepare, 0)
    lax.fori_loop(6, 8, prepare, 0)
    lax.fori_loop(9, 12, prepare, 0)
    load_rs.wait()

    for k in range(PANELS):
        place = inverse_place(k)
        answer = dot3(split(work[k]), (ahi[place], alo[place]), ((1,), (1,)))
        x = split(answer)
        for m in range(k + 1, PANELS):
            place = block_place(k, m)
            work[m] = work[m] - dot3(x, (ahi[place], alo[place]), ((1,), (0,)))

        @pl.when(row == k)
        def _(answer=answer):
            out[pl.ds(0, NB), :] = answer.T

        for half in (0, 1):
            xhi[k, half] = x[0][:, half * HALF : (half + 1) * HALF]
            xlo[k, half] = x[1][:, half * HALF : (half + 1) * HALF]
        if k == 1:
            peer_arrivals(5)
            peer_arrivals(6)
            peer_arrivals(7)
    for d, part in ((0, ONE), (1, TWO)):
        origin = origin_of(8, d)
        from_peer(origin, 8, d, part).wait_recv()
        peer_to_sibling(origin, 8, d, part).start()

    def update(block, parts):
        lanes = pl.ds(pl.multiple_of(block * NB, NB), NB)

        def factor(half, k):
            return jnp.concatenate(
                [big[0, half, :, k, :, lanes], big[1, half, :, k, :, lanes]], axis=1
            ).reshape(HALF, NB)

        total = None
        for group in parts:
            f = jnp.concatenate([factor(half, k) for half, k in group], axis=0)
            x = tuple(
                jnp.concatenate([ref[k, half] for half, k in group], axis=1) for ref in (xhi, xlo)
            )
            term = dot3(x, split(f), ((1,), (0,)))
            total = term if total is None else total + term
        rows = pl.ds(pl.multiple_of(block * NB, NB), NB)
        out[rows, :] = out[rows, :] - total.T

    def all_blocks(parts):
        def blocks(block, carry):
            update(block, parts)
            return carry

        lax.fori_loop(1 - row // OWNERS, 4, blocks, 0)

    own_half = big.at[1 - q, xh]
    pltpu.make_async_copy(own_half, own_half, sib_r.at[1]).wait()
    all_blocks((((xh, 0), (xh, 1)), ((xh, 2), (xh, 3))))
    rest = big.at[1 - q, 1 - xh, :, REST]
    pltpu.make_async_copy(rest, rest, sib_r.at[3]).wait()
    all_blocks((((1 - xh, 0), (1 - xh, 1)), ((1 - xh, 2), (1 - xh, 3))))

    def left(kind, ref):
        pltpu.make_async_copy(ref, ref, send.at[kind]).wait()

    most = pl.ds(0, NZ - 1)
    left(RING, big.at[q, xh, most])
    left(TREE, small.at[q, y, most])
    left(Y, small.at[q, pl.ds(0, 2)])
    left(RELAY, small.at[q, 0])
    left(X, big.at[q, xh, :, REST])
    left(SIB, big.at[q, xh])
    left(SIB_SMALL, small.at[q])
    left(SIB_PEER, big.at[q, 1 - xh, :, REST])

    for k in (1, 2, 3):

        @pl.when(row == k)
        def _(k=k):
            src, dst = chain(k, xh)
            for i, device in enumerate(alike):
                remote(src, dst, ch_s.at[i], ch_r.at[xh], device).wait_send()

    for quarter in (0, 1):

        @pl.when(y == quarter)
        def _(quarter=quarter):
            src, dst = inverse_part(quarter, xh)
            remote(src, dst, ch_s.at[3], ch_r.at[2], peer).wait_send()

    for part in (0, 1):
        ref = b_half(bvec.at[0], part)
        for i in range(3):
            remote(ref, ref, b_s.at[i, part], b_r.at[0, part], peer).wait_send()

    @pl.when(row < OWNERS)
    def _():
        for part in (0, 1):
            b_cross(0, part).wait_send()


def per_device(right_side, factor_panels, inverses):
    rows, columns = right_side.shape
    dma = pltpu.SemaphoreType.DMA
    return pl.pallas_call(
        kernel,
        name="solve",
        out_shape=pltpu.VMEM((rows, columns), F32),
        in_specs=[pl.BlockSpec(memory_space=pltpu.HBM)] * 3,
        out_specs=pl.BlockSpec(memory_space=pltpu.VMEM),
        scratch_shapes=[
            pltpu.VMEM((2, 2, NZ, PANELS, 4, rows), F32),
            pltpu.VMEM((2, 4, NZ, 2, SLOTS, 4, NB), F32),
            pltpu.VMEM((OWNERS, NB, columns), F32),
            pltpu.VMEM((PANELS, 2, columns, HALF), BF16),
            pltpu.VMEM((PANELS, 2, columns, HALF), BF16),
            pltpu.VMEM((4 * SLOTS, NB, NB), BF16),
            pltpu.VMEM((4 * SLOTS, NB, NB), BF16),
            dma((8,)),
            dma((2, 8, len(CHUNKS))),
            dma((2, 8, 2)),
            dma((3, 2, 9, 2)),
            dma((2, 9)),
            dma((4,)),
            dma((4,)),
            dma((4,)),
            dma((4, 2)),
            dma((4, 2)),
            dma((2,)),
        ],
        compiler_params=pltpu.CompilerParams(
            collective_id=0, has_side_effects=True, vmem_limit_bytes=62 << 20
        ),
        cost_estimate=pl.CostEstimate(flops=1 << 31, bytes_accessed=8 << 20, transcendentals=0),
    )(right_side, factor_panels, inverses)


def solution(mesh):
    in_specs = (P("row", "col"), P(None, "col", "row"), P(None, "col", None))
    return jax.shard_map(
        per_device, mesh=mesh, in_specs=in_specs, out_specs=P("row", "col"), check_vma=False
    )
```

```python
import jax
import jax.numpy as jnp
from jax import lax
from jax.experimental import pallas as pl
from jax.experimental.pallas import tpu as pltpu
from jax.sharding import PartitionSpec as P

MESH = pl.DeviceIdType.MESH
NZ = 16
PANELS = 4
OWNERS = 4
NB = 256
HALF = 128
CHUNKS = ((0, 2), (2, 2))
SLOTS = 3
BF16 = jnp.bfloat16
F32 = jnp.float32

def block_place(m, k):
    return SLOTS * k + m


def inverse_place(k):
    return k + k // 3


RING, TREE, Y, RELAY, X, SIB, SIB_SMALL, SIB_PEER = range(8)


def split(value):
    high = value.astype(BF16)
    low = (value - high.astype(F32)).astype(BF16)
    return high, low


def dot3(a, b, dims):
    def one(p, q):
        return lax.dot_general(p, q, (dims, ((), ())), preferred_element_type=F32)

    return one(a[0], b[0]) + (one(a[0], b[1]) + one(a[1], b[0]))


def kernel(
    rs_hbm, fac, inv, out,
    big, small, bvec, xhi, xlo, ahi, alo,
    send, ring_r, tree_r, y_r, x_r, sib_r,
    ch_s, ch_r, b_s, b_r, loc_s,
):
    row = lax.axis_index("row")
    col = lax.axis_index("col")
    y = row % 4
    xh, z, q = col // 32, (col // 2) % NZ, col % 2

    def at(row_to, xh_to, z_to, q_to):
        return (row_to, (xh_to * NZ + z_to) * 2 + q_to)

    def along_z(hop):
        return at(row, xh, (z + NZ + hop) % NZ, q)

    def along_y(hop):
        return at((row // 4) * 4 + (y + 4 + hop) % 4, xh, z, q)

    sibling = at(row, xh, z, 1 - q)
    peer = at(row, 1 - xh, z, q)
    alike = [at((row + 4 * (i % 2)) % 8, (xh + i // 2) % 2, z, q) for i in (1, 2, 3)]
    across_y = [along_y(1), along_y(-1)]
    before, after, over = (y + 3) % 4, (y + 1) % 4, (y + 2) % 4

    own_big = pltpu.make_async_copy(fac, big.at[q, xh, z], loc_s.at[1])
    own_big.start()
    load_rs = pltpu.make_async_copy(rs_hbm, out, loc_s.at[0])
    load_rs.start()

    barrier = pltpu.get_barrier_semaphore()
    greet = [along_z(hop) for hop in (1, -1, 2, -2)] + [sibling] + alike + across_y
    for device in greet:
        pl.semaphore_signal(barrier, inc=1, device_id=device, device_id_type=MESH)
    pl.semaphore_wait(barrier, len(greet))

    def remote(src, dst, send, recv, device):
        return pltpu.make_async_remote_copy(
            src_ref=src, dst_ref=dst, send_sem=send, recv_sem=recv,
            device_id=device, device_id_type=MESH,
        )

    def origin_of(distance, d):
        return (z + NZ - distance) % NZ if d == 0 else (z + distance) % NZ

    def chunk(origin, c):
        return big.at[q, xh, origin, pl.ds(CHUNKS[c][0], CHUNKS[c][1])]

    def hop_to(hop, d):
        return along_z(hop if d == 0 else -hop)

    def grow(held, hop, d, c):
        ref = chunk(origin_of(held, d), c)
        return remote(ref, ref, send.at[RING], ring_r.at[d, held + hop - 1, c], hop_to(hop, d))

    def arrival(distance, d, c):
        ref = chunk(origin_of(distance, d), c)
        return remote(ref, ref, send.at[RING], ring_r.at[d, distance - 1, c], hop_to(1, d))

    def to_sibling(origin, slot, d, c):
        ref = chunk(origin, c)
        return remote(ref, ref, send.at[SIB], sib_r.at[1], sibling)

    def to_peer(origin, slot, d, c):
        ref = chunk(origin, c)
        return remote(ref, ref, send.at[X], x_r.at[d, slot], peer)

    def peer_part(origin, part):
        return big.at[q, 1 - xh, origin, part]

    def from_peer(origin, slot, d, part):
        ref = peer_part(origin, part)
        return remote(ref, ref, send.at[SIB_PEER], x_r.at[d, slot], peer)

    def peer_to_sibling(origin, slot, d, part):
        ref = peer_part(origin, part)
        return remote(ref, ref, send.at[SIB_PEER], sib_r.at[3], sibling)

    REST, ONE, TWO = pl.ds(0, 4), pl.ds(0, 2), pl.ds(2, 2)

    def last_leaves(d, c):
        return (d == 1) == (CHUNKS[c][0] >= 2)

    LAST = [(d, c) for c in range(len(CHUNKS)) for d in (0, 1) if last_leaves(d, c)]

    def hand_on(distance, d, c):
        origin = origin_of(distance, d)
        to_peer(origin, distance, d, c).start()
        to_sibling(origin, distance, d, c).start()

    def take_end(distance, d, c):
        arrival(distance, d, c).wait_recv()
        hand_on(distance, d, c)

    def peer_arrivals(step):
        for d in (0, 1):
            origin = origin_of(step, d)
            from_peer(origin, step, d, REST).wait_recv()
            peer_to_sibling(origin, step, d, REST).start()

    def small_part(quarter, origin, h):
        return small.at[q, quarter, origin, h]

    def tree(held, hop, d, h):
        ref = small_part(y, origin_of(held, d), h)
        to = held + hop - 1
        return remote(ref, ref, send.at[TREE], tree_r.at[d, to, h], along_z(hop if d == 0 else -hop))

    def small_arrival(distance, d, h):
        ref = small_part(y, origin_of(distance, d), h)
        return remote(ref, ref, send.at[TREE], tree_r.at[d, distance - 1, h], along_z(1))

    def small_to_y(distance, d, h, i):
        ref = small_part(y, origin_of(distance, d), h)
        return remote(ref, ref, send.at[Y], y_r.at[i, d, distance, h], across_y[i])

    def small_to_sibling(distance, d, h):
        ref = small_part(y, origin_of(distance, d), h)
        return remote(ref, ref, send.at[SIB_SMALL], sib_r.at[0], sibling)

    def y_arrival(distance, d, h, i):
        ref = small_part((before, after, over)[i], origin_of(distance, d), h)
        return remote(ref, ref, send.at[SIB_SMALL], y_r.at[i, d, distance, h], sibling)

    def y_to_sibling(distance, d, h, i):
        ref = small_part((before, after, over)[i], origin_of(distance, d), h)
        return remote(ref, ref, send.at[SIB_SMALL], sib_r.at[0], sibling)

    def relay(distance, d, h):
        ref = small_part((before, after)[h], origin_of(distance, d), h)
        return remote(ref, ref, send.at[RELAY], y_r.at[2, d, distance, h], across_y[h])

    def spread(distance, d, h):
        for i in (0, 1):
            small_to_y(distance, d, h, i).start()
        small_to_sibling(distance, d, h).start()

    def take_odd(distance, d, h):
        small_arrival(distance, d, h).wait_recv()
        spread(distance, d, h)

    def take_y(distance, d, h):
        for i in (0, 1):
            y_arrival(distance, d, h, i).wait_recv()
            if i == h:
                relay(distance, d, h).start()
            y_to_sibling(distance, d, h, i).start()

    def take_over(distance, d, h):
        y_arrival(distance, d, h, 2).wait_recv()
        y_to_sibling(distance, d, h, 2).start()

    def chain(k, h):
        return fac.at[pl.ds(0, k), :, pl.ds(0, NB)], small.at[q, k, z, h, pl.ds(0, k)]

    for k in (1, 2, 3):

        @pl.when(row == k)
        def _(k=k):
            src, dst = chain(k, xh)
            for i, device in enumerate(alike):
                remote(src, dst, ch_s.at[i], ch_r.at[xh], device).start()
            pltpu.make_async_copy(src, dst, ch_r.at[xh]).start()

    def inverse_part(quarter, h):
        src = inv.at[pl.ds(0, 3)] if quarter == 0 else inv.at[pl.ds(3, 1)]
        return src, small.at[q, quarter, z, h, pl.ds(0, 3) if quarter == 0 else pl.ds(1, 1)]

    for quarter in (0, 1):

        @pl.when(y == quarter)
        def _(quarter=quarter):
            src, dst = inverse_part(quarter, xh)
            remote(src, dst, ch_s.at[3], ch_r.at[2], peer).start()
            pltpu.make_async_copy(src, dst, ch_r.at[3]).start()

    @pl.when((y == 1) | (y == 2))
    def _():
        for h in (0, 1):
            small[q, y, z, h, 2] = jnp.zeros((4, NB), F32)

    def b_half(ref, part):
        return ref.at[pl.ds(part * HALF, HALF)]

    def b_cross(k, part):
        return remote(
            b_half(rs_hbm, part), b_half(bvec.at[k], part), b_s.at[3, part], b_r.at[k, part], at(k + 4, xh, z, q)
        )

    for k in range(OWNERS):

        @pl.when(row == k)
        def _(k=k):
            for part in (0, 1):
                b_cross(k, part).start()

    own_big.wait()
    for c in range(len(CHUNKS)):
        for d in (0, 1):
            grow(0, 2, d, c).start()
            grow(0, 1, d, c).start()
    for c in range(len(CHUNKS)):
        to_peer(z, 0, 0, c).start()
        to_sibling(z, 0, 0, c).start()

    for k in range(OWNERS):

        @pl.when(row == k)
        def _(k=k):
            for part in (0, 1):
                for i in (0, 1):
                    remote(
                        b_half(rs_hbm, part), b_half(bvec.at[k], part), b_s.at[i, part], b_r.at[k, part], across_y[i]
                    ).start()
                pltpu.make_async_copy(
                    b_half(rs_hbm, part), b_half(bvec.at[k], part), b_r.at[k, part]
                ).start()

    def b_wait(k, part):
        pltpu.make_async_copy(b_half(rs_hbm, part), b_half(bvec.at[k], part), b_r.at[k, part]).wait()

    def forward_b(part):
        for k in range(OWNERS):

            @pl.when(row == OWNERS + k)
            def _(k=k):
                b_wait(k, part)
                ref = b_half(bvec.at[k], part)
                for i in (0, 1):
                    remote(ref, ref, b_s.at[i, part], b_r.at[k, part], across_y[i]).start()

    def relay_b(part):
        k = (before, after)[part]
        b_wait(k, part)
        ref = b_half(bvec.at[k], part)
        remote(ref, ref, b_s.at[2, part], b_r.at[k, part], across_y[part]).start()

    for quarter in (0, 1):

        @pl.when(y == quarter)
        def _(quarter=quarter):
            for sem, h in ((ch_r.at[3], xh), (ch_r.at[2], 1 - xh)):
                src, dst = inverse_part(quarter, h)
                pltpu.make_async_copy(src, dst, sem).wait()

    for k in (1, 2, 3):

        @pl.when(y == k)
        def _(k=k):
            for h in (0, 1):
                src, dst = chain(k, h)
                pltpu.make_async_copy(src, dst, ch_r.at[h]).wait()

    for h in (0, 1):
        for d in (0, 1):
            tree(0, 2, d, h).start()
            tree(0, 1, d, h).start()
        spread(0, 0, h)

    forward_b(0)

    def steps(j, carry):
        for h in (0, 1):
            for d in (0, 1):
                small_arrival(2 * j, d, h).wait_recv()
                if h == d:
                    tree(2 * j, 2, d, h).start()
                else:

                    @pl.when(j < 3)
                    def _(d=d, h=h):
                        tree(2 * j, 2, d, h).start()

                tree(2 * j, 1, d, h).start()
                spread(2 * j, d, h)
        for c in range(len(CHUNKS)):
            for d in (0, 1):
                arrival(2 * j, d, c).wait_recv()
                if last_leaves(d, c):
                    grow(2 * j, 2, d, c).start()
                else:

                    @pl.when(j < 3)
                    def _(d=d, c=c):
                        grow(2 * j, 2, d, c).start()

                grow(2 * j, 1, d, c).start()
                hand_on(2 * j, d, c)
        for h in (0, 1):
            for d in (0, 1):
                take_odd(2 * j - 1, d, h)

        @pl.when(j == 1)
        def _():
            from_peer(z, 0, 0, REST).wait_recv()
            peer_to_sibling(z, 0, 0, REST).start()
            forward_b(1)
            for h in (0, 1):
                take_y(0, 0, h)

        @pl.when(j > 1)
        def _():
            for h in (0, 1):
                for d in (0, 1):
                    take_y(2 * j - 3, d, h)
                    take_y(2 * j - 2, d, h)

        @pl.when(j == 2)
        def _():
            for part in (0, 1):
                relay_b(part)
            for h in (0, 1):
                take_over(0, 0, h)

        @pl.when(j == 3)
        def _():
            for h in (0, 1):
                for d in (0, 1):
                    take_over(1, d, h)
                    take_over(2, d, h)

        for c in range(len(CHUNKS)):
            for d in (0, 1):
                take_end(2 * j - 1, d, c)

        @pl.when(j > 1)
        def _():
            peer_arrivals(2 * j - 3)
            peer_arrivals(2 * j - 2)

        return carry

    lax.fori_loop(1, 4, steps, 0)
    for h in (0, 1):
        take_odd(8, h, h)
    for h in (0, 1):
        for d in (0, 1):
            take_odd(7, d, h)
    for h in (0, 1):
        for d in (0, 1):
            take_y(5, d, h)
            take_y(6, d, h)
    for d, c in LAST:
        take_end(8, d, c)
    for h in (0, 1):
        for d in (0, 1):
            take_over(3, d, h)
            take_over(4, d, h)
    for h in (0, 1):
        take_y(8, h, h)
        for d in (0, 1):
            take_y(7, d, h)
    for c in range(len(CHUNKS)):
        for d in (0, 1):
            take_end(7, d, c)
    for h in (0, 1):
        for d in (0, 1):
            take_over(5, d, h)
            take_over(6, d, h)
    for h in (0, 1):
        take_over(8, h, h)
        for d in (0, 1):
            take_over(7, d, h)

    @pl.when(row < OWNERS)
    def _():
        for part in (0, 1):
            b_wait(y, part)

    b_wait(before, 1)
    b_wait(after, 0)
    for part in (0, 1):
        b_wait(over, part)

    work = [bvec[k].T for k in range(PANELS)]

    sib_small = small.at[1 - q]
    pltpu.make_async_copy(sib_small, sib_small, sib_r.at[0]).wait()

    def prepare(place, carry):
        quarter, slot = place // SLOTS, place % SLOTS
        for half in (0, 1):
            value = jnp.concatenate(
                [small[0, quarter, :, half, slot], small[1, quarter, :, half, slot]], axis=1
            ).reshape(HALF, NB)
            ahi[place, pl.ds(half * HALF, HALF), :], alo[place, pl.ds(half * HALF, HALF), :] = split(value)
        return carry

    lax.fori_loop(0, 5, prepare, 0)
    lax.fori_loop(6, 8, prepare, 0)
    lax.fori_loop(9, 12, prepare, 0)
    load_rs.wait()

    for k in range(PANELS):
        place = inverse_place(k)
        answer = dot3(split(work[k]), (ahi[place], alo[place]), ((1,), (1,)))
        x = split(answer)
        for m in range(k + 1, PANELS):
            place = block_place(k, m)
            work[m] = work[m] - dot3(x, (ahi[place], alo[place]), ((1,), (0,)))

        @pl.when(row == k)
        def _(answer=answer):
            out[pl.ds(0, NB), :] = answer.T

        for half in (0, 1):
            xhi[k, half] = x[0][:, half * HALF : (half + 1) * HALF]
            xlo[k, half] = x[1][:, half * HALF : (half + 1) * HALF]
        if k == 1:
            peer_arrivals(5)
            peer_arrivals(6)
            peer_arrivals(7)
    for d, part in ((0, ONE), (1, TWO)):
        origin = origin_of(8, d)
        from_peer(origin, 8, d, part).wait_recv()
        peer_to_sibling(origin, 8, d, part).start()

    def update(block, parts):
        lanes = pl.ds(pl.multiple_of(block * NB, NB), NB)

        def factor(half, k):
            return jnp.concatenate(
                [big[0, half, :, k, :, lanes], big[1, half, :, k, :, lanes]], axis=1
            ).reshape(HALF, NB)

        total = None
        for group in parts:
            f = jnp.concatenate([factor(half, k) for half, k in group], axis=0)
            x = tuple(
                jnp.concatenate([ref[k, half] for half, k in group], axis=1) for ref in (xhi, xlo)
            )
            term = dot3(x, split(f), ((1,), (0,)))
            total = term if total is None else total + term
        rows = pl.ds(pl.multiple_of(block * NB, NB), NB)
        out[rows, :] = out[rows, :] - total.T

    def all_blocks(parts):
        def blocks(block, carry):
            update(block, parts)
            return carry

        lax.fori_loop(1 - row // OWNERS, 4, blocks, 0)

    own_half = big.at[1 - q, xh]
    pltpu.make_async_copy(own_half, own_half, sib_r.at[1]).wait()
    all_blocks((((xh, 0), (xh, 1)), ((xh, 2), (xh, 3))))
    rest = big.at[1 - q, 1 - xh, :, REST]
    pltpu.make_async_copy(rest, rest, sib_r.at[3]).wait()
    all_blocks((((1 - xh, 0), (1 - xh, 1)), ((1 - xh, 2), (1 - xh, 3))))

    def left(kind, ref):
        pltpu.make_async_copy(ref, ref, send.at[kind]).wait()

    most = pl.ds(0, NZ - 1)
    left(RING, big.at[q, xh, most])
    left(TREE, small.at[q, y, most])
    left(Y, small.at[q, pl.ds(0, 2)])
    left(RELAY, small.at[q, 0])
    left(X, big.at[q, xh, :, REST])
    left(SIB, big.at[q, xh])
    left(SIB_SMALL, small.at[q])
    left(SIB_PEER, big.at[q, 1 - xh, :, REST])

    for k in (1, 2, 3):

        @pl.when(row == k)
        def _(k=k):
            src, dst = chain(k, xh)
            for i, device in enumerate(alike):
                remote(src, dst, ch_s.at[i], ch_r.at[xh], device).wait_send()

    for quarter in (0, 1):

        @pl.when(y == quarter)
        def _(quarter=quarter):
            src, dst = inverse_part(quarter, xh)
            remote(src, dst, ch_s.at[3], ch_r.at[2], peer).wait_send()

    for part in (0, 1):
        ref = b_half(bvec.at[0], part)
        for i in range(3):
            remote(ref, ref, b_s.at[i, part], b_r.at[0, part], peer).wait_send()

    @pl.when(row < OWNERS)
    def _():
        for part in (0, 1):
            b_cross(0, part).wait_send()


def per_device(right_side, factor_panels, inverses):
    rows, columns = right_side.shape
    dma = pltpu.SemaphoreType.DMA
    return pl.pallas_call(
        kernel,
        name="solve",
        out_shape=pltpu.VMEM((rows, columns), F32),
        in_specs=[pl.BlockSpec(memory_space=pltpu.HBM)] * 3,
        out_specs=pl.BlockSpec(memory_space=pltpu.VMEM),
        scratch_shapes=[
            pltpu.VMEM((2, 2, NZ, PANELS, 4, rows), F32),
            pltpu.VMEM((2, 4, NZ, 2, SLOTS, 4, NB), F32),
            pltpu.VMEM((OWNERS, NB, columns), F32),
            pltpu.VMEM((PANELS, 2, columns, HALF), BF16),
            pltpu.VMEM((PANELS, 2, columns, HALF), BF16),
            pltpu.VMEM((4 * SLOTS, NB, NB), BF16),
            pltpu.VMEM((4 * SLOTS, NB, NB), BF16),
            dma((8,)),
            dma((2, 8, len(CHUNKS))),
            dma((2, 8, 2)),
            dma((3, 2, 9, 2)),
            dma((2, 9)),
            dma((4,)),
            dma((4,)),
            dma((4,)),
            dma((4, 2)),
            dma((4, 2)),
            dma((2,)),
        ],
        compiler_params=pltpu.CompilerParams(
            collective_id=0, has_side_effects=True, vmem_limit_bytes=62 << 20
        ),
        cost_estimate=pl.CostEstimate(flops=1 << 31, bytes_accessed=8 << 20, transcendentals=0),
    )(right_side, factor_panels, inverses)


def solution(mesh):
    in_specs = (P("row", "col"), P(None, "col", "row"), P(None, "col", None))
    return jax.shard_map(
        per_device, mesh=mesh, in_specs=in_specs, out_specs=P("row", "col"), check_vma=False
    )
```
